128 devices in a mesh: row: 8 (over y_lo, x), col: 16 (over y_hi, z, core).
Axes of the slice: x: 4, y: 4 (y_hi: 2, y_lo: 2; y = y_hi * 2 + y_lo), z: 4, core: 2. Of those that a mesh axis runs over, the one named last changes fastest.
Arguments:
- pair_rep: bfloat16 [512, 512, 128], P('row', 'col'), may hold values from -40 to 40
- residue_mask: int32 [512], replicated, may hold values 0 or 1
- chain_index: int32 [512], replicated, may hold values from 0 to 5, never falling along the last dimension, each value on 1 to 256 neighbouring positions
- mul_in: bfloat16 [128, 512], replicated, may hold values from -0.5 to 0.5
- mul_gate: bfloat16 [128, 128], replicated, may hold values from -0.5 to 0.5
- mul_out: bfloat16 [128, 128], replicated, may hold values from -0.5 to 0.5
- att_in: bfloat16 [128, 512], replicated, may hold values from -0.5 to 0.5
- att_bias: bfloat16 [128, 4], replicated, may hold values from -28 to 28
- chain_bias: float32 [4], replicated, may hold values from -5 to 5
- att_out: bfloat16 [128, 128], replicated, may hold values from -0.5 to 0.5
- trans_up: bfloat16 [128, 512], replicated, may hold values from -0.5 to 0.5
- trans_down: bfloat16 [512, 128], replicated, may hold values from -0.25 to 0.25
Outputs:
- new_pair: bfloat16 [512, 512, 128], P('row', 'col')
The draws below stay inside these ranges and needn't reach their ends.
All inputs are finite; a program needn't handle non-finite values.
Results may differ from the reference program's by a relative error of at most 0.04.
The reference program's roundings to bfloat16 on the way count: a program that leaves them out, or rounds other values in their place, can miss the bound.
Values may be sent and summed in bfloat16 or wider, within the bound.
A program may use at most 128 MiB of HBM per device.

```python
import math
import jax
import jax.numpy as jnp
import numpy as np
from jax import lax

CP = 128
CMUL = 128
HEADS = 4
HEAD = 32
TRANS = 512
N = 512


def draw_pair_rep(key, part):
    key = jax.random.fold_in(key, 11)
    values_all = jnp.clip(jax.random.normal(key, (N, N, CP), jnp.float32), -6.0, 6.0)
    return values_all.astype(jnp.bfloat16)


def draw_att_bias(key, part):
    key = jax.random.fold_in(key, 12)
    values_all = jnp.clip(jax.random.normal(key, (CP, HEADS), jnp.float32), -6.0, 6.0) * (4.0 * CP ** (-0.5))
    return values_all.astype(jnp.bfloat16)


def touch_ends(array, key, least, top_value):
    index_at = [jax.random.randint(jax.random.fold_in(key, axis), (), 0, length) for axis, length in enumerate(array.shape)]
    widest = array.shape.index(max(array.shape))
    neighbour = index_at[:widest] + [(index_at[widest] + 1) % array.shape[widest]] + index_at[widest + 1:]
    return array.at[tuple(index_at)].set(least).at[tuple(neighbour)].set(top_value)


def profile(number_of, total, limit, lean):
    weights = [(1 << 20) // math.isqrt(standing ** lean) + 1 for standing in range(2, number_of + 1)]
    spare, counts = total - limit - (number_of - 1), [1] * (number_of - 1)
    while spare > 0:
        candidates = [i for i in range(number_of - 1) if counts[i] < limit]
        mass, left = sum([weights[i] for i in candidates]), spare
        for i in candidates:
            extra = min(limit - counts[i], max(1, left * weights[i] // mass), spare)
            counts[i] = counts[i] + extra
            spare = spare - extra
    return np.array([limit] + counts)


def uneven(rng, number_of, total, bound, slope):
    if number_of == 2:
        one = jax.random.randint(rng, (), max(1, total - bound), min(bound, total - 1) + 1)
        return jnp.stack([one, total - one])
    sizes = jnp.asarray(profile(number_of, total, bound, slope), jnp.int32)
    pairs = (number_of - 1) // 2
    source_of, taker = sizes[1:1 + 2 * pairs:2], sizes[2:2 + 2 * pairs:2]
    margin = jnp.minimum(source_of - 1, bound - taker)
    passed = jax.random.randint(jax.random.fold_in(rng, 1), (pairs,), 0, 1 << 20) % (margin + 1)
    sizes = sizes.at[1:1 + 2 * pairs:2].set(source_of - passed).at[2:2 + 2 * pairs:2].set(taker + passed)
    return sizes[jax.random.permutation(jax.random.fold_in(rng, 2), number_of)]


def bell_draw(stream_key, dims, width, bound, kind=jnp.bfloat16):
    values = width * jax.random.normal(stream_key, dims, jnp.float32)
    return jnp.clip(values, min=-bound, max=bound).astype(kind)


def setup_inputs(seed: int = 0) -> dict:
    key_list = jax.random.split(jax.random.key(seed), 13)
    return {
        "pair_rep": draw_pair_rep(jax.random.fold_in(key_list[12], 71), 0),
        "residue_mask": touch_ends((jax.random.randint(key_list[1], (N,), 0, 8) < 7).astype(jnp.int32), jax.random.fold_in(key_list[1], 1), 0, 1),
        "chain_index": jnp.searchsorted(jnp.cumsum(uneven(key_list[2], 6, N, N // 2, 1)), jnp.arange(N), side="right").astype(jnp.int32),
        "mul_in": bell_draw(key_list[3], (CP, 4 * CMUL), CP ** -0.5, 0.5),
        "mul_gate": bell_draw(key_list[4], (CP, CP), CP ** -0.5, 0.5),
        "mul_out": bell_draw(key_list[5], (CMUL, CP), CMUL ** -0.5, 0.5),
        "att_in": bell_draw(key_list[6], (CP, 4 * HEADS * HEAD), CP ** -0.5, 0.5),
        "att_bias": draw_att_bias(jax.random.fold_in(key_list[12], 71), 0),
        "chain_bias": jnp.clip(jax.random.uniform(key_list[8], (HEADS,), jnp.float32, -5.0, 5.0), -5.0, 5.0),
        "att_out": bell_draw(key_list[9], (HEADS * HEAD, CP), (HEADS * HEAD) ** -0.5, 0.5),
        "trans_up": bell_draw(key_list[10], (CP, TRANS), CP ** -0.5, 0.5),
        "trans_down": bell_draw(key_list[11], (TRANS, CP), TRANS ** -0.5, 0.25),
    }


def layer_norm(values, axis):
    values = values.astype(jnp.float32)
    average = lax.optimization_barrier(jnp.mean(values, axis=axis, keepdims=True))
    centred = values - average
    variance = lax.optimization_barrier(jnp.mean(centred * centred, axis=axis, keepdims=True))
    return centred * lax.rsqrt(variance + 1e-05)

def project(normed, weight, form):
    return jnp.einsum(form, normed.astype(jnp.float32), weight.astype(jnp.float32), precision=lax.Precision.HIGHEST)

def reference(pair_rep, residue_mask, chain_index, mul_in, mul_gate, mul_out, att_in, att_bias, chain_bias, att_out, trans_up, trans_down):
    attn_width = HEADS * HEAD
    mask_all = residue_mask.astype(jnp.float32)
    pair_mask = mask_all[:, None] * mask_all[None, :]
    normed = layer_norm(pair_rep, 2).astype(jnp.bfloat16)
    left_proj = (pair_mask * jax.nn.sigmoid(project(normed, mul_in[:, CMUL:2 * CMUL], 'ijp,pe->eij')) * project(normed, mul_in[:, :CMUL], 'ijp,pe->eij')).astype(jnp.bfloat16)
    right_proj = (pair_mask * jax.nn.sigmoid(project(normed, mul_in[:, 3 * CMUL:], 'ijp,pe->eij')) * project(normed, mul_in[:, 2 * CMUL:3 * CMUL], 'ijp,pe->eij')).astype(jnp.bfloat16)
    mix_sum = jnp.einsum('cik,cjk->cij', left_proj.astype(jnp.float32), right_proj.astype(jnp.float32), precision=lax.Precision.HIGHEST)
    mix_normed = layer_norm(mix_sum, 0).astype(jnp.bfloat16)
    gate_mul = jax.nn.sigmoid(project(normed, mul_gate, 'ijp,pq->ijq'))
    update = gate_mul * jnp.einsum('cij,cq->ijq', mix_normed.astype(jnp.float32), mul_out.astype(jnp.float32), precision=lax.Precision.HIGHEST)
    pair_one = (pair_rep.astype(jnp.float32) + update).astype(jnp.bfloat16)
    normed_two = layer_norm(pair_one, 2).astype(jnp.bfloat16)
    queries = project(normed_two, att_in[:, :attn_width], 'ijp,pe->ije').astype(jnp.bfloat16)
    key_loc = project(normed_two, att_in[:, attn_width:2 * attn_width], 'ijp,pe->ije').astype(jnp.bfloat16)
    value_loc = project(normed_two, att_in[:, 2 * attn_width:3 * attn_width], 'ijp,pe->ije').astype(jnp.bfloat16)
    gate_att = jax.nn.sigmoid(project(normed_two, att_in[:, 3 * attn_width:], 'ijp,pe->ije'))
    same_chain = (chain_index[:, None] == chain_index[None, :]).astype(jnp.float32)
    bias_table = project(normed_two, att_bias, 'jkp,ph->jhk') + chain_bias[None, :, None] * same_chain[:, None, :] + 1000000000.0 * (mask_all - 1.0)[None, None, :]
    block_len = math.gcd(N, 16)
    shaped = (N // block_len, block_len, N, HEADS, HEAD)
    score_scale = HEAD ** (-0.5)

    def one_block(items):
        query_block, key_block, value_block = items
        scores = jnp.einsum('ijhd,ikhd->ijhk', query_block, key_block, precision=lax.Precision.HIGHEST) * score_scale + bias_table[None]
        top_score = lax.optimization_barrier(jnp.max(scores, axis=-1, keepdims=True))
        weights = jnp.exp(scores - top_score)
        denominator = lax.optimization_barrier(jnp.sum(weights, axis=-1))
        rounded = weights.astype(jnp.bfloat16).astype(jnp.float32)
        weighted = jnp.einsum('ijhk,ikhd->ijhd', rounded, value_block, precision=lax.Precision.HIGHEST)
        return weighted / denominator[..., None]
    attended = lax.map(one_block, (queries.astype(jnp.float32).reshape(shaped), key_loc.astype(jnp.float32).reshape(shaped), value_loc.astype(jnp.float32).reshape(shaped)))
    attended = attended.reshape(N, N, attn_width)
    gated_out = (gate_att * attended).astype(jnp.bfloat16)
    pair_two = (pair_one.astype(jnp.float32) + project(gated_out, att_out, 'ije,eq->ijq')).astype(jnp.bfloat16)
    normed_three = layer_norm(pair_two, 2).astype(jnp.bfloat16)
    inner_act = jax.nn.relu(project(normed_three, trans_up, 'ijp,pe->ije')).astype(jnp.bfloat16)
    return (pair_two.astype(jnp.float32) + project(inner_act, trans_down, 'ije,eq->ijq')).astype(jnp.bfloat16)
```

```python
import functools
import math

import jax
import jax.numpy as jnp
from jax import lax
from jax.experimental import pallas as pl
from jax.experimental.pallas import tpu as pltpu
from jax.sharding import PartitionSpec as P

MESH = pl.DeviceIdType.MESH
F32 = jnp.float32
BF16 = jnp.bfloat16
EPS = 1e-05
LOG2E = math.log2(math.e)
ORDERS = ((0, 1, 2), (1, 2, 0), (2, 0, 1))
UNITS = ((0, 3), (3, 3), (6, 2))


def norm(values, axis):
    centred = values - jnp.mean(values, axis=axis, keepdims=True)
    variance = jnp.mean(centred * centred, axis=axis, keepdims=True)
    return (centred * lax.rsqrt(variance + EPS)).astype(BF16)


def dot(a, b, ca=1, cb=0):
    return lax.dot_general(a, b, (((ca,), (cb,)), ((), ())), preferred_element_type=F32)


def one_hot(shape, hit):
    rows = lax.broadcasted_iota(jnp.int32, shape, 0)
    cols = lax.broadcasted_iota(jnp.int32, shape, 1)
    return jnp.where(hit(rows, cols), 1.0, 0.0).astype(BF16)


def kernel(
    pair_ref, mask_ref, chain_ref, mul_in_ref, mul_gate_ref, mul_out_ref, att_in_ref, att_bias_ref, chain_bias_ref,
    att_out_ref, up_ref, down_ref, out_ref,
    pair_f, lr_f, lr_s, lr_r, at_l, at_r, m_f, m_s, m_r, pair_rows, one_all, bias_own, bias0, bias1, bias2, table, same,
    keys, values, queries, gates, one_mine, out_s, out_r,
    ready, local, send, recv, gather_send, gather_recv,
):
    row, col = lax.axis_index("row"), lax.axis_index("col")
    me = row * 16 + col
    core = lax.rem(col, 2)
    place = (lax.rem(row, 4), col // 8 * 2 + row // 4, lax.rem(col // 2, 4))
    biases = (bias0, bias1, bias2)

    def device_at(c):
        return (lax.rem(c[1], 2) * 4 + c[0], c[1] // 2 * 8 + c[2] * 2 + core)

    def signal_row(sem):
        def one(s, carry):
            pl.semaphore_signal(sem, inc=1, device_id=(lax.rem(row + s, 8), col), device_id_type=MESH)
            return carry
        lax.fori_loop(1, 8, one, 0)

    def signal_col(sem):
        def one(s, carry):
            pl.semaphore_signal(sem, inc=1, device_id=(row, lax.rem(col + s, 16)), device_id_type=MESH)
            return carry
        lax.fori_loop(1, 16, one, 0)

    def remote(src, dst, which, target):
        return pltpu.make_async_remote_copy(src, dst, send.at[which], recv.at[which], device_id=target, device_id_type=MESH)

    barrier = pltpu.get_barrier_semaphore()
    signal_row(barrier)
    signal_col(barrier)

    mask = mask_ref[...].astype(F32)
    pair_f[...] = pair_ref[...].astype(F32).reshape(2048, 128)
    pick_rows = one_hot((512, 128), lambda a, b: a == row * 64 + lax.rem(b, 64))
    row_mask = dot(jnp.broadcast_to(mask, (16, 512)).astype(BF16), pick_rows)
    place_col = lax.broadcasted_iota(jnp.int32, (16, 512), 1) - (col * 32 + 2 * lax.broadcasted_iota(jnp.int32, (16, 512), 0))
    even = jnp.sum(jnp.where(place_col == 0, mask, 0.0), axis=1, keepdims=True)
    odd = jnp.sum(jnp.where(place_col == 1, mask, 0.0), axis=1, keepdims=True)
    lanes16 = lax.broadcasted_iota(jnp.int32, (16, 128), 1)
    pair_mask = jnp.where(lanes16 < 64, even, odd) * row_mask
    mul_in_t = mul_in_ref[...].T
    for step in range(8):
        parts = [pair_f[pl.ds(4 * step + u, 64, stride=32), :] for u in range(4)]
        normed = norm(jnp.concatenate(parts, axis=0).T, 0)
        projected = dot(mul_in_t, normed)
        masks = jnp.concatenate([pair_mask[2 * step : 2 * step + 1], pair_mask[2 * step + 1 : 2 * step + 2]], axis=1)
        left = masks * jax.nn.sigmoid(projected[128:256]) * projected[:128]
        right = masks * jax.nn.sigmoid(projected[384:]) * projected[256:384]
        for v in range(2):
            lr_f[pl.ds(2 * step + v, 128, stride=32), :] = left[:, v * 128 : v * 128 + 128]
            lr_f[pl.ds(16 + 2 * step + v, 128, stride=32), :] = right[:, v * 128 : v * 128 + 128]
    lr_s[...] = lr_f[...].reshape(128, 2, 16, 128).astype(BF16)

    pl.semaphore_wait(barrier, 22)
    signal_row(ready)
    pl.semaphore_wait(ready, 7)

    def to_all(src, dst, which):
        def one(s, carry):
            r, c = lax.rem(row + s // 16, 8), lax.rem(col + lax.rem(s, 16), 16)
            remote(src.at[r * 16 + c], dst.at[me], which, (r, c)).start()
            return carry
        lax.fori_loop(1, 128, one, 0)
        pltpu.make_async_copy(src.at[me], dst.at[me], local.at[which]).start()

    def all_here(src, dst, which):
        pltpu.make_async_copy(src.at[me], dst.at[me], local.at[which]).wait()
        whole = remote(src.at[pl.ds(0, 127)], dst.at[pl.ds(0, 127)], which, (row, col))
        whole.wait_send()
        whole.wait_recv()

    to_all(lr_s, lr_r, 0)

    def send_pair(s, carry):
        c = lax.rem(col + s, 16)
        remote(pair_ref.at[pl.ds(4 * c, 4)], pair_rows.at[col], 1, (row, c)).start()
        return carry
    lax.fori_loop(1, 16, send_pair, 0)
    pltpu.make_async_copy(pair_ref.at[pl.ds(4 * col, 4)], pair_rows.at[col], local.at[1]).start()

    def place_left(a, b):
        k, il, r, g = b // 128, lax.rem(b // 32, 4), lax.rem(b // 16, 2), lax.rem(b, 16)
        return a == r * 128 + k * 64 + 4 * g + il

    def place_right(a, b):
        k, r, i = b // 128, lax.rem(b // 64, 2), lax.rem(b, 64)
        return a == r * 128 + k * 64 + i

    orders = (one_hot((256, 256), place_left), one_hot((256, 256), place_right))
    head_rows = lax.broadcasted_iota(jnp.int32, (16, 512), 0)
    chains = jnp.where(head_rows == chain_ref[...], 1.0, 0.0).astype(BF16)
    mine = one_hot((256, 512), lambda a, b: b == a // 4 * 8 + core * 4 + lax.rem(a, 4))
    chains_mine = dot(chains, mine, 1, 1).astype(BF16)
    same[...] = dot(chains_mine.T, chains)

    all_here(lr_s, lr_r, 0)
    for side, at in ((0, at_l), (1, at_r)):
        for rp in range(4):
            here = [lr_r[(2 * rp + o) * 16 : (2 * rp + o + 1) * 16, side].reshape(256, 128) for o in range(2)]
            turned = dot(jnp.concatenate(here, axis=1), orders[side]).astype(BF16)
            at[0:256, rp * 128 : rp * 128 + 128] = turned[:, :128]
            at[256:512, rp * 128 : rp * 128 + 128] = turned[:, 128:]
    for rp in range(4):
        product = dot(at_l[:, rp * 128 : rp * 128 + 128].T, at_r[...])
        for il in range(4):
            for jt in range(4):
                m_f[pl.ds(rp * 512 + il * 4 + jt, 32, stride=16), :] = product[il * 32 : il * 32 + 32, jt * 128 : jt * 128 + 128]
    m_s[...] = m_f[...].reshape(128, 16, 128).astype(BF16)
    to_all(m_s, m_r, 2)

    pltpu.make_async_copy(pair_ref.at[pl.ds(0, 4)], pair_rows.at[0], local.at[1]).wait()
    whole = remote(pair_rows.at[pl.ds(0, 15)], pair_rows.at[pl.ds(0, 15)], 1, (row, col))
    whole.wait_send()
    whole.wait_recv()
    all_here(m_s, m_r, 2)

    m_f[...] = m_r[...].astype(F32).reshape(2048, 128)
    bias_in = jnp.concatenate([att_bias_ref[...].astype(F32).T, jnp.zeros((4, 128), F32)], axis=0).astype(BF16)
    for il in range(4):
        for jt in range(4):
            mix = norm(m_f[pl.ds(il * 4 + jt, 128, stride=16), :], 0)
            update = dot(mix, mul_out_ref[...], 0, 0)
            pair = pair_rows[4 * jt : 4 * jt + 4, il].reshape(128, 128).astype(F32)
            gate = jax.nn.sigmoid(dot(norm(pair, 1), mul_gate_ref[...]))
            one = (pair + gate * update).astype(BF16)
            one_all[core * 4 + il, jt * 128 : jt * 128 + 128] = one
            bias = dot(bias_in, norm(one.astype(F32), 1), 1, 1)
            for h in range(4):
                bias_own[h // 2 * 4 + jt, h % 2 * 4 + il : h % 2 * 4 + il + 1, :] = bias[h : h + 1]

    sibling = (row, col + 1 - 2 * core)
    swap = remote(one_all.at[pl.ds(core * 4, 4)], one_all.at[pl.ds(core * 4, 4)], 3, sibling)
    swap.start()

    def slab(o, phase, full):
        a, b, c = (place[axis] for axis in ORDERS[o])
        if phase == 0:
            return biases[o].at[c, b, pl.ds(0, 3)] if full else biases[o].at[c, b, a]
        if phase == 1:
            return biases[o].at[c, pl.ds(0, 3)] if full else biases[o].at[c, b]
        return biases[o].at[pl.ds(0, 3)] if full else biases[o].at[c]

    def gather_start(phase):
        for o in range(3):
            axis = ORDERS[o][phase]
            for s in (1, 3, 2):
                there = list(place)
                there[axis] = lax.rem(place[axis] + s, 4)
                ref = slab(o, phase, False)
                pltpu.make_async_remote_copy(
                    ref, ref, gather_send.at[o, phase], gather_recv.at[o, phase], device_id=device_at(there), device_id_type=MESH
                ).start()

    def gather_wait(phase):
        for o in range(3):
            ref = slab(o, phase, True)
            whole = pltpu.make_async_remote_copy(
                ref, ref, gather_send.at[o, phase], gather_recv.at[o, phase], device_id=(row, col), device_id_type=MESH
            )
            whole.wait_send()
            whole.wait_recv()

    for o in range(3):
        a, b, c = (place[axis] for axis in ORDERS[o])
        first, count = UNITS[o]
        biases[o][c, b, a] = bias_own[first : first + count]
    gather_start(0)

    heads = lax.broadcasted_iota(jnp.int32, (256, 128), 1) // 32

    def project(i):
        one = one_all[i]
        normed = norm(one.astype(F32), 1)
        normed_mine = dot(mine, normed).astype(BF16)
        one_mine[i] = dot(mine, one)
        kv = dot(normed, att_in_ref[:, 128:384]).astype(BF16)
        keys[i] = kv[:, :128]
        values[i] = kv[:, 128:]
        query = dot(normed_mine, att_in_ref[:, :128])
        for h in range(4):
            queries[i, h * 256 : h * 256 + 256] = jnp.where(heads == h, query, 0.0).astype(BF16)
        gates[i] = jax.nn.sigmoid(dot(normed_mine, att_in_ref[:, 384:]))

    def project_own(n, carry):
        project(core * 4 + n)
        return carry

    def project_other(n, carry):
        project(4 - core * 4 + n)
        return carry

    lax.fori_loop(0, 2, project_own, 0)
    gather_wait(0)
    gather_start(1)
    lax.fori_loop(2, 4, project_own, 0)
    gather_wait(1)
    gather_start(2)
    swap.wait()
    lax.fori_loop(0, 4, project_other, 0)
    gather_wait(2)

    mask_term = 1000000000.0 * (mask - 1.0)
    upper = lax.broadcasted_iota(jnp.int32, (8, 128), 0) < 4

    def build(n, carry):
        x, y = lax.rem(n // 2, 4), lax.rem(n, 2) * 2 + n // 8
        for u in range(8):
            o = 0 if u < 3 else 1 if u < 6 else 2
            lanes = pl.ds(u % 4 * 128, 128)
            for zp in range(2):
                tiles = []
                for z in (2 * zp, 2 * zp + 1):
                    at = (x, y, z)
                    a, b, c = (at[axis] for axis in ORDERS[o])
                    tiles.append(biases[o][c, b, a, u - UNITS[o][0]])
                rows = pl.ds(pl.multiple_of(n * 16 + zp * 8, 8), 8)
                together = same[rows, lanes]
                mixed = (
                    jnp.where(upper, tiles[0], pltpu.roll(tiles[1], 4, 0)),
                    jnp.where(upper, pltpu.roll(tiles[0], 4, 0), tiles[1]),
                )
                for h2 in range(2):
                    h = u // 4 * 2 + h2
                    value = mixed[h2] + chain_bias_ref[0, h] * together + mask_term[:, u % 4 * 128 : u % 4 * 128 + 128]
                    table[h, rows, lanes] = value * LOG2E
        return carry

    lax.fori_loop(0, 16, build, 0)

    scale = 32 ** (-0.5) * LOG2E

    def attend(i, carry):
        total = jnp.zeros((256, 128), F32)
        for h in range(4):
            scores = dot(queries[i, h * 256 : h * 256 + 256], keys[i], 1, 1) * scale + table[h]
            weights = jnp.exp2(scores - jnp.max(scores, axis=1, keepdims=True))
            denominator = jnp.sum(weights, axis=1, keepdims=True)
            weighted = dot(weights.astype(BF16), values[i])
            total = total + jnp.where(heads == h, weighted / denominator, 0.0)
        gated = (gates[i] * total).astype(BF16)
        two = (one_mine[i] + dot(gated, att_out_ref[...])).astype(BF16)
        two_f = two.astype(F32)
        inner = jnp.maximum(dot(norm(two_f, 1), up_ref[...]), 0.0).astype(BF16)
        result = (two_f + dot(inner, down_ref[...])).astype(BF16)
        out_s[:, i] = result.reshape(16, 16, 128)
        return carry

    lax.fori_loop(0, 8, attend, 0)

    def send_out(s, carry):
        c = lax.rem(col + s, 16)
        remote(out_s.at[c], out_r.at[col], 4, (row, c)).start()
        return carry
    lax.fori_loop(1, 16, send_out, 0)
    keep = pltpu.make_async_copy(out_s.at[col], out_r.at[col], local.at[4])
    keep.start()
    keep.wait()
    whole = remote(out_s.at[pl.ds(0, 15)], out_r.at[pl.ds(0, 15)], 4, (row, col))
    whole.wait_send()
    whole.wait_recv()

    def place_out(a, b):
        il, group, which, jl = a // 32, lax.rem(a // 8, 4), lax.rem(a // 4, 2), lax.rem(a, 4)
        return b == which * 128 + il * 16 + group * 4 + jl

    back = one_hot((256, 256), place_out)
    for chip in range(8):
        block = out_r[2 * chip : 2 * chip + 2].reshape(256, 128)
        out_ref[8 * chip : 8 * chip + 8] = dot(back, block).astype(BF16).reshape(8, 32, 128)


def body(pair_rep, residue_mask, chain_index, mul_in, mul_gate, mul_out, att_in, att_bias, chain_bias, att_out, trans_up, trans_down):
    vmem = pl.BlockSpec(memory_space=pltpu.VMEM)
    specs = [vmem] * 12
    specs[8] = pl.BlockSpec(memory_space=pltpu.SMEM)
    sem = pltpu.SemaphoreType
    return pl.pallas_call(
        kernel,
        out_shape=jax.ShapeDtypeStruct(pair_rep.shape, BF16),
        in_specs=specs,
        out_specs=vmem,
        scratch_shapes=[
            pltpu.VMEM((2048, 128), F32),
            pltpu.VMEM((4096, 128), F32),
            pltpu.VMEM((128, 2, 16, 128), BF16),
            pltpu.VMEM((128, 2, 16, 128), BF16),
            pltpu.VMEM((512, 512), BF16),
            pltpu.VMEM((512, 512), BF16),
            pltpu.VMEM((2048, 128), F32),
            pltpu.VMEM((128, 16, 128), BF16),
            pltpu.VMEM((128, 16, 128), BF16),
            pltpu.VMEM((16, 4, 32, 128), BF16),
            pltpu.VMEM((8, 512, 128), BF16),
            pltpu.VMEM((8, 8, 128), F32),
            pltpu.VMEM((4, 4, 4, 3, 8, 128), F32),
            pltpu.VMEM((4, 4, 4, 3, 8, 128), F32),
            pltpu.VMEM((4, 4, 4, 2, 8, 128), F32),
            pltpu.VMEM((4, 256, 512), F32),
            pltpu.VMEM((256, 512), F32),
            pltpu.VMEM((8, 512, 128), BF16),
            pltpu.VMEM((8, 512, 128), BF16),
            pltpu.VMEM((8, 1024, 128), BF16),
            pltpu.VMEM((8, 256, 128), F32),
            pltpu.VMEM((8, 256, 128), F32),
            pltpu.VMEM((16, 8, 16, 128), BF16),
            pltpu.VMEM((16, 8, 16, 128), BF16),
            sem.REGULAR,
            sem.DMA((5,)),
            sem.DMA((5,)),
            sem.DMA((5,)),
            sem.DMA((3, 3)),
            sem.DMA((3, 3)),
        ],
        compiler_params=pltpu.CompilerParams(collective_id=0, has_side_effects=True, vmem_limit_bytes=48 * 1024 * 1024),
    )(
        pair_rep, residue_mask.reshape(1, -1), chain_index.reshape(1, -1), mul_in, mul_gate, mul_out, att_in, att_bias,
        chain_bias.reshape(1, -1), att_out, trans_up, trans_down,
    )


def solution(mesh):
    in_specs = (P("row", "col", None),) + (P(),) * 11
    return jax.shard_map(body, mesh=mesh, in_specs=in_specs, out_specs=P("row", "col", None), check_vma=False)
```

```python
import functools
import math

import jax
import jax.numpy as jnp
from jax import lax
from jax.experimental import pallas as pl
from jax.experimental.pallas import tpu as pltpu
from jax.sharding import PartitionSpec as P

MESH = pl.DeviceIdType.MESH
F32 = jnp.float32
BF16 = jnp.bfloat16
EPS = 1e-05
LOG2E = math.log2(math.e)
ORDERS = ((0, 1, 2), (1, 2, 0), (2, 0, 1), (0, 1, 2), (1, 2, 0))
OUT_ROWS = ((0, 4), (4, 2), (6, 2))


def norm(values, axis):
    centred = values - jnp.mean(values, axis=axis, keepdims=True)
    variance = jnp.mean(centred * centred, axis=axis, keepdims=True)
    return (centred * lax.rsqrt(variance + EPS)).astype(BF16)


def dot(a, b, ca=1, cb=0):
    return lax.dot_general(a, b, (((ca,), (cb,)), ((), ())), preferred_element_type=F32)


def one_hot(shape, hit):
    rows = lax.broadcasted_iota(jnp.int32, shape, 0)
    cols = lax.broadcasted_iota(jnp.int32, shape, 1)
    return jnp.where(hit(rows, cols), 1.0, 0.0).astype(BF16)


def kernel(
    pair_in, mask_in, chain_in, mul_in_in, mul_gate_in, mul_out_in, att_in_in, att_bias_in, chain_bias_ref,
    att_out_in, up_in, down_in, out_ref,
    pair_ref, mask_ref, chain_ref, mul_in_ref, mul_gate_ref, mul_out_ref, att_in_ref, att_bias_ref, att_out_ref, up_ref, down_ref,
    pair_f, lr_f, lr_s, lr_r, at_l, at_r, m_f, m_s, m_r, pair_rows, one_all, bias0, bias1, bias2, bias3, bias4, table, same,
    keys, values, queries, gates, one_mine, score_s, weight_s, total_s, out_s, out_r,
    ready, load, local, send, recv, gather_send, gather_recv,
):
    row, col = lax.axis_index("row"), lax.axis_index("col")
    me = row * 16 + col
    core = lax.rem(col, 2)
    place = (lax.rem(row, 4), col // 8 * 2 + row // 4, lax.rem(col // 2, 4))
    biases = (bias0, bias1, bias2, bias3, bias4)

    def device_at(c):
        return (lax.rem(c[1], 2) * 4 + c[0], c[1] // 2 * 8 + c[2] * 2 + core)

    def signal_row(sem):
        def one(s, carry):
            pl.semaphore_signal(sem, inc=1, device_id=(lax.rem(row + s, 8), col), device_id_type=MESH)
            return carry
        lax.fori_loop(1, 8, one, 0)

    def signal_col(sem):
        def one(s, carry):
            pl.semaphore_signal(sem, inc=1, device_id=(row, lax.rem(col + s, 16)), device_id_type=MESH)
            return carry
        lax.fori_loop(1, 16, one, 0)

    def remote(src, dst, which, target):
        return pltpu.make_async_remote_copy(src, dst, send.at[which], recv.at[which], device_id=target, device_id_type=MESH)

    loads = [
        pltpu.make_async_copy(src, dst, load.at[n])
        for n, (src, dst) in enumerate((
            (mask_in, mask_ref), (pair_in, pair_ref), (mul_in_in, mul_in_ref), (chain_in, chain_ref),
            (mul_gate_in, mul_gate_ref), (mul_out_in, mul_out_ref), (att_in_in, att_in_ref), (att_bias_in, att_bias_ref),
            (att_out_in, att_out_ref), (up_in, up_ref), (down_in, down_ref),
        ))
    ]
    for one in loads[:3]:
        one.start()
    barrier = pltpu.get_barrier_semaphore()
    signal_row(barrier)
    signal_col(barrier)
    for one in loads[3:]:
        one.start()
    for one in loads[:3]:
        one.wait()

    mask = mask_ref[...].astype(F32)
    pair_f[...] = pair_ref[...].astype(F32).reshape(2048, 128)
    pick_rows = one_hot((512, 128), lambda a, b: a == row * 64 + lax.rem(b, 64))
    row_mask = dot(jnp.broadcast_to(mask, (16, 512)).astype(BF16), pick_rows)
    place_col = lax.broadcasted_iota(jnp.int32, (16, 512), 1) - (col * 32 + 2 * lax.broadcasted_iota(jnp.int32, (16, 512), 0))
    even = jnp.sum(jnp.where(place_col == 0, mask, 0.0), axis=1, keepdims=True)
    odd = jnp.sum(jnp.where(place_col == 1, mask, 0.0), axis=1, keepdims=True)
    lanes16 = lax.broadcasted_iota(jnp.int32, (16, 128), 1)
    pair_mask = jnp.where(lanes16 < 64, even, odd) * row_mask
    mul_in_t = mul_in_ref[...].T
    for step in range(8):
        if step == 4:
            pl.semaphore_wait(barrier, 22)
            signal_row(ready)
        parts = [pair_f[pl.ds(4 * step + u, 64, stride=32), :] for u in range(4)]
        normed = norm(jnp.concatenate(parts, axis=0).T, 0)
        projected = dot(mul_in_t, normed)
        masks = jnp.concatenate([pair_mask[2 * step : 2 * step + 1], pair_mask[2 * step + 1 : 2 * step + 2]], axis=1)
        left = masks * jax.nn.sigmoid(projected[128:256]) * projected[:128]
        right = masks * jax.nn.sigmoid(projected[384:]) * projected[256:384]
        for v in range(2):
            lr_f[pl.ds(2 * step + v, 128, stride=32), :] = left[:, v * 128 : v * 128 + 128]
            lr_f[pl.ds(16 + 2 * step + v, 128, stride=32), :] = right[:, v * 128 : v * 128 + 128]
    lr_s[...] = lr_f[...].reshape(128, 2, 16, 128).astype(BF16)

    for one in loads[3:]:
        one.wait()
    pl.semaphore_wait(ready, 7)

    def to_all(src, dst, which):
        def one(s, carry):
            r, c = lax.rem(row + s // 16, 8), lax.rem(col + lax.rem(s, 16), 16)
            remote(src.at[r * 16 + c], dst.at[me], which, (r, c)).start()
            return carry
        lax.fori_loop(1, 128, one, 0)
        pltpu.make_async_copy(src.at[me], dst.at[me], local.at[which]).start()

    def all_here(src, dst, which):
        pltpu.make_async_copy(src.at[me], dst.at[me], local.at[which]).wait()
        whole = remote(src.at[pl.ds(0, 127)], dst.at[pl.ds(0, 127)], which, (row, col))
        whole.wait_send()
        whole.wait_recv()

    to_all(lr_s, lr_r, 0)

    def place_left(a, b):
        k, il, r, g = b // 128, lax.rem(b // 32, 4), lax.rem(b // 16, 2), lax.rem(b, 16)
        return a == r * 128 + k * 64 + 4 * g + il

    def place_right(a, b):
        k, r, i = b // 128, lax.rem(b // 64, 2), lax.rem(b, 64)
        return a == r * 128 + k * 64 + i

    orders = (one_hot((256, 256), place_left), one_hot((256, 256), place_right))
    head_rows = lax.broadcasted_iota(jnp.int32, (16, 512), 0)
    chains = jnp.where(head_rows == chain_ref[...], 1.0, 0.0).astype(BF16)
    mine = one_hot((256, 512), lambda a, b: b == a // 4 * 8 + core * 4 + lax.rem(a, 4))
    chains_mine = dot(chains, mine, 1, 1).astype(BF16)
    same[...] = dot(chains_mine.T, chains)

    all_here(lr_s, lr_r, 0)

    def send_pair(s, carry):
        c = lax.rem(col + s, 16)
        remote(pair_ref.at[pl.ds(4 * c, 4)], pair_rows.at[col], 1, (row, c)).start()
        return carry
    lax.fori_loop(1, 16, send_pair, 0)
    pltpu.make_async_copy(pair_ref.at[pl.ds(4 * col, 4)], pair_rows.at[col], local.at[1]).start()

    for side, at in ((0, at_l), (1, at_r)):
        for rp in range(4):
            here = [lr_r[(2 * rp + o) * 16 : (2 * rp + o + 1) * 16, side].reshape(256, 128) for o in range(2)]
            turned = dot(jnp.concatenate(here, axis=1), orders[side]).astype(BF16)
            at[0:256, rp * 128 : rp * 128 + 128] = turned[:, :128]
            at[256:512, rp * 128 : rp * 128 + 128] = turned[:, 128:]
    for rp in range(4):
        product = dot(at_l[:, rp * 128 : rp * 128 + 128].T, at_r[...])
        for il in range(4):
            for jt in range(4):
                m_f[pl.ds(rp * 512 + il * 4 + jt, 32, stride=16), :] = product[il * 32 : il * 32 + 32, jt * 128 : jt * 128 + 128]
    m_s[...] = m_f[...].reshape(128, 16, 128).astype(BF16)
    to_all(m_s, m_r, 2)

    pltpu.make_async_copy(pair_ref.at[pl.ds(0, 4)], pair_rows.at[0], local.at[1]).wait()
    whole = remote(pair_rows.at[pl.ds(0, 15)], pair_rows.at[pl.ds(0, 15)], 1, (row, col))
    whole.wait_send()
    whole.wait_recv()

    def pair_tile(jt, il):
        return pair_rows[4 * jt : 4 * jt + 4, il].reshape(128, 128).astype(F32)

    for jt in range(4):
        for il in range(4):
            at = (il * 4 + jt) * 128
            pair_f[at : at + 128] = jax.nn.sigmoid(dot(norm(pair_tile(jt, il), 1), mul_gate_ref[...]))
    all_here(m_s, m_r, 2)

    def slab(o, phase, full):
        a, b, c = (place[axis] for axis in ORDERS[o])
        if phase == 0:
            return biases[o].at[c, b, pl.ds(0, 3)] if full else biases[o].at[c, b, a]
        if phase == 1:
            return biases[o].at[c, pl.ds(0, 3)] if full else biases[o].at[c, b]
        return biases[o].at[pl.ds(0, 3)] if full else biases[o].at[c]

    early, late = (0, 1, 2), (3, 4)

    def gather_start(phase, which):
        for s in (1, 3, 2):
            for o in which:
                axis = ORDERS[o][phase]
                there = list(place)
                there[axis] = lax.rem(place[axis] + s, 4)
                ref = slab(o, phase, False)
                pltpu.make_async_remote_copy(
                    ref, ref, gather_send.at[o, phase], gather_recv.at[o, phase], device_id=device_at(there), device_id_type=MESH
                ).start()

    def gather_wait(phase, which):
        for o in which:
            ref = slab(o, phase, True)
            whole = pltpu.make_async_remote_copy(
                ref, ref, gather_send.at[o, phase], gather_recv.at[o, phase], device_id=(row, col), device_id_type=MESH
            )
            whole.wait_send()
            whole.wait_recv()

    m_f[...] = m_r[...].astype(F32).reshape(2048, 128)
    bias_in = jnp.concatenate([att_bias_ref[...].astype(F32), jnp.zeros((4, 128), F32)], axis=0).astype(BF16)
    for jt in range(4):
        for il in range(4):
            at = il * 4 + jt
            mix = norm(m_f[pl.ds(at, 128, stride=16), :], 0)
            update = dot(mix, mul_out_ref[...], 0, 0)
            one = (pair_tile(jt, il) + pair_f[at * 128 : at * 128 + 128] * update).astype(BF16)
            one_all[core * 4 + il, jt * 128 : jt * 128 + 128] = one
            bias = dot(bias_in, norm(one.astype(F32), 1), 1, 1)
            for h in range(4):
                o, slot = (jt, h // 2) if jt < 3 else (3 + h // 2, 0)
                a, b, c = (place[axis] for axis in ORDERS[o])
                biases[o][c, b, a, slot, h % 2 * 4 + il : h % 2 * 4 + il + 1, :] = bias[h : h + 1]
        if jt == 2:
            gather_start(0, early)
    gather_start(0, late)
    sibling = (row, col + 1 - 2 * core)
    swap = remote(one_all.at[pl.ds(core * 4, 4)], one_all.at[pl.ds(core * 4, 4)], 3, sibling)
    swap.start()

    heads = lax.broadcasted_iota(jnp.int32, (256, 128), 1) // 32

    def project(i):
        one = one_all[i]
        normed = norm(one.astype(F32), 1)
        normed_mine = dot(mine, normed).astype(BF16)
        one_mine[i] = dot(mine, one)
        kv = dot(normed, att_in_ref[:, 128:384]).astype(BF16)
        keys[i] = kv[:, :128]
        values[i] = kv[:, 128:]
        query = dot(normed_mine, att_in_ref[:, :128])
        for h in range(4):
            queries[i, h * 256 : h * 256 + 256] = jnp.where(heads == h, query, 0.0).astype(BF16)
        gates[i] = jax.nn.sigmoid(dot(normed_mine, att_in_ref[:, 384:]))

    def project_own(n, carry):
        project(core * 4 + n)
        return carry

    def project_other(n, carry):
        project(4 - core * 4 + n)
        return carry

    lax.fori_loop(0, 2, project_own, 0)
    for group in (early, late):
        gather_wait(0, group)
        gather_start(1, group)
    lax.fori_loop(2, 4, project_own, 0)
    for group in (early, late):
        gather_wait(1, group)
        gather_start(2, group)
    swap.wait()
    lax.fori_loop(0, 4, project_other, 0)
    gather_wait(2, early)
    gather_wait(2, late)

    mask_term = 1000000000.0 * (mask - 1.0)
    upper = lax.broadcasted_iota(jnp.int32, (8, 128), 0) < 4

    def build(n, carry):
        x, y = lax.rem(n // 2, 4), lax.rem(n, 2) * 2 + n // 8
        for u in range(8):
            hp, kt = u // 4, u % 4
            o, slot = (kt, hp) if kt < 3 else (3 + hp, 0)
            lanes = pl.ds(u % 4 * 128, 128)
            for zp in range(2):
                tiles = []
                for z in (2 * zp, 2 * zp + 1):
                    at = (x, y, z)
                    a, b, c = (at[axis] for axis in ORDERS[o])
                    tiles.append(biases[o][c, b, a, slot])
                rows = pl.ds(pl.multiple_of(n * 16 + zp * 8, 8), 8)
                together = same[rows, lanes]
                mixed = (
                    jnp.where(upper, tiles[0], pltpu.roll(tiles[1], 4, 0)),
                    jnp.where(upper, pltpu.roll(tiles[0], 4, 0), tiles[1]),
                )
                for h2 in range(2):
                    h = u // 4 * 2 + h2
                    value = mixed[h2] + chain_bias_ref[0, h] * together + mask_term[:, u % 4 * 128 : u % 4 * 128 + 128]
                    table[h, rows, lanes] = value * LOG2E
        return carry

    lax.fori_loop(0, 16, build, 0)

    scale = 32 ** (-0.5) * LOG2E

    def score(i, slot):
        score_s[slot] = dot(queries[i], keys[i], 1, 1)

    def soften(slot):
        for n in range(16):
            rows = slice(n * 64, n * 64 + 64)
            scores = score_s[slot, rows] * scale + table[n // 4, n % 4 * 64 : n % 4 * 64 + 64]
            weights = jnp.exp2(scores - jnp.max(scores, axis=1, keepdims=True))
            total_s[slot, rows] = jnp.broadcast_to(jnp.sum(weights, axis=1, keepdims=True), (64, 128))
            weight_s[slot, rows] = weights.astype(BF16)

    def finish(i, slot):
        weighted = dot(weight_s[slot], values[i]) / total_s[slot]
        total = jnp.zeros((256, 128), F32)
        for h in range(4):
            total = total + jnp.where(heads == h, weighted[h * 256 : h * 256 + 256], 0.0)
        gated = (gates[i] * total).astype(BF16)
        two = (one_mine[i] + dot(gated, att_out_ref[...])).astype(BF16)
        two_f = two.astype(F32)
        inner = jnp.maximum(dot(norm(two_f, 1), up_ref[...]), 0.0).astype(BF16)
        result = (two_f + dot(inner, down_ref[...])).astype(BF16)
        out_s[:, i] = result.reshape(16, 16, 128)

    def send_out(part):
        first, count = OUT_ROWS[part]
        rows = pl.ds(first, count)

        def one(s, carry):
            c = lax.rem(col + s, 16)
            remote(out_s.at[c, rows], out_r.at[col, rows], 4 + part, (row, c)).start()
            return carry
        lax.fori_loop(1, 16, one, 0)
        pltpu.make_async_copy(out_s.at[col, rows], out_r.at[col, rows], local.at[4 + part]).start()

    score(0, 0)
    for i in range(8):
        if i < 7:
            score(i + 1, (i + 1) % 2)
        soften(i % 2)
        if i > 0:
            finish(i - 1, (i - 1) % 2)
        for part in range(2):
            if i == OUT_ROWS[part + 1][0]:
                send_out(part)
    finish(7, 1)
    send_out(2)
    for part in range(3):
        rows = pl.ds(*OUT_ROWS[part])
        pltpu.make_async_copy(out_s.at[col, rows], out_r.at[col, rows], local.at[4 + part]).wait()
        whole = remote(out_s.at[pl.ds(0, 15), rows], out_r.at[pl.ds(0, 15), rows], 4 + part, (row, col))
        whole.wait_send()
        whole.wait_recv()

    def place_out(a, b):
        il, group, which, jl = a // 32, lax.rem(a // 8, 4), lax.rem(a // 4, 2), lax.rem(a, 4)
        return b == which * 128 + il * 16 + group * 4 + jl

    back = one_hot((256, 256), place_out)
    for chip in range(8):
        block = out_r[2 * chip : 2 * chip + 2].reshape(256, 128)
        out_ref[8 * chip : 8 * chip + 8] = dot(back, block).astype(BF16).reshape(8, 32, 128)


def body(pair_rep, residue_mask, chain_index, mul_in, mul_gate, mul_out, att_in, att_bias, chain_bias, att_out, trans_up, trans_down):
    vmem = pl.BlockSpec(memory_space=pltpu.VMEM)
    specs = [pl.BlockSpec(memory_space=pl.ANY)] * 12
    specs[8] = pl.BlockSpec(memory_space=pltpu.SMEM)
    sem = pltpu.SemaphoreType
    args = (
        pair_rep, residue_mask.reshape(1, -1), chain_index.reshape(1, -1), mul_in, mul_gate, mul_out, att_in, att_bias.T,
        chain_bias.reshape(1, -1), att_out, trans_up, trans_down,
    )
    return pl.pallas_call(
        kernel,
        out_shape=jax.ShapeDtypeStruct(pair_rep.shape, BF16),
        in_specs=specs,
        out_specs=vmem,
        scratch_shapes=[pltpu.VMEM(a.shape, a.dtype) for n, a in enumerate(args) if n != 8]
        + [
            pltpu.VMEM((2048, 128), F32),
            pltpu.VMEM((4096, 128), F32),
            pltpu.VMEM((128, 2, 16, 128), BF16),
            pltpu.VMEM((128, 2, 16, 128), BF16),
            pltpu.VMEM((512, 512), BF16),
            pltpu.VMEM((512, 512), BF16),
            pltpu.VMEM((2048, 128), F32),
            pltpu.VMEM((128, 16, 128), BF16),
            pltpu.VMEM((128, 16, 128), BF16),
            pltpu.VMEM((16, 4, 32, 128), BF16),
            pltpu.VMEM((8, 512, 128), BF16),
            pltpu.VMEM((4, 4, 4, 2, 8, 128), F32),
            pltpu.VMEM((4, 4, 4, 2, 8, 128), F32),
            pltpu.VMEM((4, 4, 4, 2, 8, 128), F32),
            pltpu.VMEM((4, 4, 4, 1, 8, 128), F32),
            pltpu.VMEM((4, 4, 4, 1, 8, 128), F32),
            pltpu.VMEM((4, 256, 512), F32),
            pltpu.VMEM((256, 512), F32),
            pltpu.VMEM((8, 512, 128), BF16),
            pltpu.VMEM((8, 512, 128), BF16),
            pltpu.VMEM((8, 1024, 128), BF16),
            pltpu.VMEM((8, 256, 128), F32),
            pltpu.VMEM((8, 256, 128), F32),
            pltpu.VMEM((2, 1024, 512), F32),
            pltpu.VMEM((2, 1024, 512), BF16),
            pltpu.VMEM((2, 1024, 128), F32),
            pltpu.VMEM((16, 8, 16, 128), BF16),
            pltpu.VMEM((16, 8, 16, 128), BF16),
            sem.REGULAR,
            sem.DMA((11,)),
            sem.DMA((7,)),
            sem.DMA((7,)),
            sem.DMA((7,)),
            sem.DMA((5, 3)),
            sem.DMA((5, 3)),
        ],
        compiler_params=pltpu.CompilerParams(collective_id=0, has_side_effects=True, vmem_limit_bytes=56 * 1024 * 1024),
    )(*args)


def solution(mesh):
    in_specs = (P("row", "col", None),) + (P(),) * 11
    return jax.shard_map(body, mesh=mesh, in_specs=in_specs, out_specs=P("row", "col", None), check_vma=False)
```

```python
import functools
import math

import jax
import jax.numpy as jnp
from jax import lax
from jax.experimental import pallas as pl
from jax.experimental.pallas import tpu as pltpu
from jax.sharding import PartitionSpec as P

MESH = pl.DeviceIdType.MESH
F32 = jnp.float32
BF16 = jnp.bfloat16
EPS = 1e-05
LOG2E = math.log2(math.e)
ORDERS = ((0, 1, 2), (1, 2, 0), (2, 0, 1), (1, 2, 0), (0, 1, 2), (2, 0, 1))
WHERE = {(0, 0): (0, 0), (1, 0): (0, 1), (0, 1): (1, 0), (1, 1): (2, 0), (0, 2): (3, 0), (1, 2): (3, 1), (0, 3): (4, 0), (1, 3): (5, 0)}


def norm(values, axis):
    centred = values - jnp.mean(values, axis=axis, keepdims=True)
    variance = jnp.mean(centred * centred, axis=axis, keepdims=True)
    return (centred * lax.rsqrt(variance + EPS)).astype(BF16)


def dot(a, b, ca=1, cb=0):
    return lax.dot_general(a, b, (((ca,), (cb,)), ((), ())), preferred_element_type=F32)


def one_hot(shape, hit):
    rows = lax.broadcasted_iota(jnp.int32, shape, 0)
    cols = lax.broadcasted_iota(jnp.int32, shape, 1)
    return jnp.where(hit(rows, cols), 1.0, 0.0).astype(BF16)


def kernel(
    pair_in, mask_in, chain_in, mul_in_in, mul_gate_in, mul_out_in, att_in_in, att_bias_in, chain_bias_ref,
    att_out_in, up_in, down_in, out_ref,
    pair_ref, mask_ref, chain_ref, mul_in_ref, mul_gate_ref, mul_out_ref, att_in_ref, att_bias_ref, att_out_ref, up_ref, down_ref,
    pair_f, lr_f, lr_s, lr_r, at_l, at_r, m_f, m_s, m_r, pair_rows, one_all, normed_all, bias0, bias1, bias2, bias3, bias4, bias5, table, same,
    keys, values, queries, gates, one_mine, score_s, weight_s, total_s, gated_s, out_s, out_r,
    ready, load, local, send, recv, gather_send, gather_recv,
):
    row, col = lax.axis_index("row"), lax.axis_index("col")
    me = row * 16 + col
    core = lax.rem(col, 2)
    place = (lax.rem(row, 4), col // 8 * 2 + row // 4, lax.rem(col // 2, 4))
    biases = (bias0, bias1, bias2, bias3, bias4, bias5)

    def device_at(c):
        return (lax.rem(c[1], 2) * 4 + c[0], c[1] // 2 * 8 + c[2] * 2 + core)

    def signal_row(sem):
        def one(s, carry):
            pl.semaphore_signal(sem, inc=1, device_id=(lax.rem(row + s, 8), col), device_id_type=MESH)
            return carry
        lax.fori_loop(1, 8, one, 0)

    def signal_col(sem):
        def one(s, carry):
            pl.semaphore_signal(sem, inc=1, device_id=(row, lax.rem(col + s, 16)), device_id_type=MESH)
            return carry
        lax.fori_loop(1, 16, one, 0)

    def remote(src, dst, which, target):
        return pltpu.make_async_remote_copy(src, dst, send.at[which], recv.at[which], device_id=target, device_id_type=MESH)

    loads = [
        pltpu.make_async_copy(src, dst, load.at[n])
        for n, (src, dst) in enumerate((
            (mask_in, mask_ref), (pair_in, pair_ref), (mul_in_in, mul_in_ref), (chain_in, chain_ref),
            (mul_gate_in, mul_gate_ref), (mul_out_in, mul_out_ref), (att_in_in, att_in_ref), (att_bias_in, att_bias_ref),
            (att_out_in, att_out_ref), (up_in, up_ref), (down_in, down_ref),
        ))
    ]
    for one in loads[:3]:
        one.start()
    barrier = pltpu.get_barrier_semaphore()
    signal_row(barrier)
    signal_col(barrier)
    for one in loads[3:]:
        one.start()
    for one in loads[:3]:
        one.wait()

    def send_pair(part):
        rows = pl.ds(2 * part, 2)

        def one(s, carry):
            c = lax.rem(col + s, 16)
            remote(pair_ref.at[pl.ds(4 * c + 2 * part, 2)], pair_rows.at[col, rows], 6 + part, (row, c)).start()
            return carry
        lax.fori_loop(1, 16, one, 0)
        pltpu.make_async_copy(pair_ref.at[pl.ds(4 * col + 2 * part, 2)], pair_rows.at[col, rows], local.at[6 + part]).start()

    mask = mask_ref[...].astype(F32)
    pair_f[...] = pair_ref[...].astype(F32).reshape(2048, 128)
    pick_rows = one_hot((512, 128), lambda a, b: a == row * 64 + lax.rem(b, 64))
    row_mask = dot(jnp.broadcast_to(mask, (16, 512)).astype(BF16), pick_rows)
    place_col = lax.broadcasted_iota(jnp.int32, (16, 512), 1) - (col * 32 + 2 * lax.broadcasted_iota(jnp.int32, (16, 512), 0))
    even = jnp.sum(jnp.where(place_col == 0, mask, 0.0), axis=1, keepdims=True)
    odd = jnp.sum(jnp.where(place_col == 1, mask, 0.0), axis=1, keepdims=True)
    lanes16 = lax.broadcasted_iota(jnp.int32, (16, 128), 1)
    pair_mask = jnp.where(lanes16 < 64, even, odd) * row_mask
    mul_in_t = mul_in_ref[...].T
    for step in range(2):
        if step == 1:
            pl.semaphore_wait(barrier, 22)
            signal_row(ready)
            send_pair(0)
        parts = [pair_f[pl.ds(16 * step + u, 64, stride=32), :] for u in range(16)]
        normed = norm(jnp.concatenate(parts, axis=0).T, 0)
        projected = dot(mul_in_t, normed)
        masks = jnp.concatenate([pair_mask[8 * step + v : 8 * step + v + 1] for v in range(8)], axis=1)
        left = masks * jax.nn.sigmoid(projected[128:256]) * projected[:128]
        right = masks * jax.nn.sigmoid(projected[384:]) * projected[256:384]
        for v in range(8):
            lr_f[pl.ds(8 * step + v, 128, stride=32), :] = left[:, v * 128 : v * 128 + 128]
            lr_f[pl.ds(16 + 8 * step + v, 128, stride=32), :] = right[:, v * 128 : v * 128 + 128]
    lr_s[...] = lr_f[...].reshape(128, 2, 16, 128).astype(BF16)

    for one in loads[3:]:
        one.wait()
    pl.semaphore_wait(ready, 7)

    def to_all(src, dst, which):
        def one(s, carry):
            r, c = lax.rem(row + s // 16, 8), lax.rem(col + lax.rem(s, 16), 16)
            remote(src.at[r * 16 + c], dst.at[me], which, (r, c)).start()
            return carry
        lax.fori_loop(1, 128, one, 0)
        pltpu.make_async_copy(src.at[me], dst.at[me], local.at[which]).start()

    def all_here(src, dst, which):
        pltpu.make_async_copy(src.at[me], dst.at[me], local.at[which]).wait()
        whole = remote(src.at[pl.ds(0, 127)], dst.at[pl.ds(0, 127)], which, (row, col))
        whole.wait_send()
        whole.wait_recv()

    to_all(lr_s, lr_r, 0)

    def place_left(a, b):
        k, il, r, g = b // 128, lax.rem(b // 32, 4), lax.rem(b // 16, 2), lax.rem(b, 16)
        return a == r * 128 + k * 64 + 4 * g + il

    def place_right(a, b):
        k, r, i = b // 128, lax.rem(b // 64, 2), lax.rem(b, 64)
        return a == r * 128 + k * 64 + i

    orders = (one_hot((256, 256), place_left), one_hot((256, 256), place_right))
    head_rows = lax.broadcasted_iota(jnp.int32, (16, 512), 0)
    chains = jnp.where(head_rows == chain_ref[...], 1.0, 0.0).astype(BF16)
    mine = one_hot((256, 512), lambda a, b: b == a // 4 * 8 + core * 4 + lax.rem(a, 4))
    chains_mine = dot(chains, mine, 1, 1).astype(BF16)
    same[...] = dot(chains_mine.T, chains)

    all_here(lr_s, lr_r, 0)

    send_pair(1)
    for side, at in ((0, at_l), (1, at_r)):
        here = [
            jnp.concatenate([lr_r[(2 * rp + o) * 16 : (2 * rp + o + 1) * 16, side].reshape(256, 128) for o in range(2)], axis=1)
            for rp in range(4)
        ]
        turned = dot(jnp.concatenate(here, axis=0), orders[side]).astype(BF16)
        for rp in range(4):
            for k in range(2):
                at[k * 256 : k * 256 + 256, rp * 128 : rp * 128 + 128] = turned[rp * 256 : rp * 256 + 256, k * 128 : k * 128 + 128]
    product = dot(at_l[...], at_r[...], 0, 0)
    for rp in range(4):
        for il in range(4):
            at = rp * 128 + il * 32
            for jt in range(4):
                m_f[pl.ds(rp * 512 + il * 4 + jt, 32, stride=16), :] = product[at : at + 32, jt * 128 : jt * 128 + 128]
    m_s[...] = m_f[...].reshape(128, 16, 128).astype(BF16)
    to_all(m_s, m_r, 2)

    for part in range(2):
        rows = pl.ds(2 * part, 2)
        pltpu.make_async_copy(pair_ref.at[pl.ds(0, 2)], pair_rows.at[0, rows], local.at[6 + part]).wait()
        whole = remote(pair_rows.at[pl.ds(0, 15), rows], pair_rows.at[pl.ds(0, 15), rows], 6 + part, (row, col))
        whole.wait_send()
        whole.wait_recv()

    def pair_block(half):
        blocks = [pair_rows[8 * half : 8 * half + 8, il].reshape(256, 128) for il in range(4)]
        return jnp.concatenate(blocks, axis=0).astype(F32)

    for half in range(2):
        pair_f[half * 1024 : half * 1024 + 1024] = jax.nn.sigmoid(dot(norm(pair_block(half), 1), mul_gate_ref[...]))
    all_here(m_s, m_r, 2)

    def slab(o, phase, full):
        a, b, c = (place[axis] for axis in ORDERS[o])
        if phase == 0:
            return biases[o].at[c, b, pl.ds(0, 3)] if full else biases[o].at[c, b, a]
        if phase == 1:
            return biases[o].at[c, pl.ds(0, 3)] if full else biases[o].at[c, b]
        return biases[o].at[pl.ds(0, 3)] if full else biases[o].at[c]

    early, late = (0, 1, 2), (3, 4, 5)

    def gather_start(phase, which):
        for s in (1, 3, 2):
            for o in which:
                axis = ORDERS[o][phase]
                there = list(place)
                there[axis] = lax.rem(place[axis] + s, 4)
                ref = slab(o, phase, False)
                pltpu.make_async_remote_copy(
                    ref, ref, gather_send.at[o, phase], gather_recv.at[o, phase], device_id=device_at(there), device_id_type=MESH
                ).start()

    def gather_wait(phase, which):
        for o in which:
            ref = slab(o, phase, True)
            whole = pltpu.make_async_remote_copy(
                ref, ref, gather_send.at[o, phase], gather_recv.at[o, phase], device_id=(row, col), device_id_type=MESH
            )
            whole.wait_send()
            whole.wait_recv()

    m_f[...] = m_r[...].astype(F32).reshape(2048, 128)
    bias_in = jnp.concatenate([att_bias_ref[...].astype(F32), jnp.zeros((4, 128), F32)], axis=0).astype(BF16)
    for half in range(2):
        tiles = [m_f[pl.ds(il * 4 + 2 * half + t, 128, stride=16), :] for il in range(4) for t in range(2)]
        update = dot(norm(jnp.concatenate(tiles, axis=1), 0), mul_out_ref[...], 0, 0)
        one = (pair_block(half) + pair_f[half * 1024 : half * 1024 + 1024] * update).astype(BF16)
        normed = norm(one.astype(F32), 1)
        bias = dot(bias_in, normed, 1, 1)
        for il in range(4):
            one_all[core * 4 + il, half * 256 : half * 256 + 256] = one[il * 256 : il * 256 + 256]
            normed_all[il, half * 256 : half * 256 + 256] = normed[il * 256 : il * 256 + 256]
            for t in range(2):
                lanes = slice((il * 2 + t) * 128, (il * 2 + t) * 128 + 128)
                for h in range(4):
                    o, slot = WHERE[h // 2, 2 * half + t]
                    a, b, c = (place[axis] for axis in ORDERS[o])
                    biases[o][c, b, a, slot, h % 2 * 4 + il : h % 2 * 4 + il + 1, :] = bias[h : h + 1, lanes]
        if half == 0:
            gather_start(0, early)
    gather_start(0, late)
    sibling = (row, col + 1 - 2 * core)
    swap = remote(one_all.at[pl.ds(core * 4, 4)], one_all.at[pl.ds(core * 4, 4)], 3, sibling)
    swap.start()

    heads = lax.broadcasted_iota(jnp.int32, (256, 128), 1) // 32

    def project(first, normed):
        four = pl.ds(first, 4)
        kv = dot(normed, att_in_ref[:, 128:384]).astype(BF16)
        keys[four] = kv[:, :128].reshape(4, 512, 128)
        values[four] = kv[:, 128:].reshape(4, 512, 128)
        picked = []
        for n in range(4):
            both = dot(mine, jnp.concatenate([normed[n * 512 : n * 512 + 512], one_all[first + n]], axis=1))
            picked.append(both[:, :128].astype(BF16))
            one_mine[first + n] = both[:, 128:]
        picked = jnp.concatenate(picked, axis=0)
        query = dot(picked, att_in_ref[:, :128])
        for n in range(4):
            for h in range(4):
                queries[first + n, h * 256 : h * 256 + 256] = jnp.where(heads == h, query[n * 256 : n * 256 + 256], 0.0).astype(BF16)
        gates[four] = jax.nn.sigmoid(dot(picked, att_in_ref[:, 384:])).reshape(4, 256, 128)

    project(core * 4, normed_all[...].reshape(2048, 128))
    for group in (early, late):
        gather_wait(0, group)
        gather_start(1, group)
    swap.wait()
    other = 4 - core * 4
    project(other, norm(one_all[pl.ds(other, 4)].reshape(2048, 128).astype(F32), 1))
    for group in (early, late):
        gather_wait(1, group)
        gather_start(2, group)

    mask_term = 1000000000.0 * (mask - 1.0)
    upper = lax.broadcasted_iota(jnp.int32, (8, 128), 0) < 4

    def build(half, n, carry):
        x, y = lax.rem(n // 2, 4), lax.rem(n, 2) * 2 + n // 8
        for hp, kt in ((0, 2 * half), (1, 2 * half), (0, 2 * half + 1), (1, 2 * half + 1)):
            o, slot = WHERE[hp, kt]
            lanes = pl.ds(kt * 128, 128)
            for zp in range(2):
                tiles = []
                for z in (2 * zp, 2 * zp + 1):
                    at = (x, y, z)
                    a, b, c = (at[axis] for axis in ORDERS[o])
                    tiles.append(biases[o][c, b, a, slot])
                rows = pl.ds(pl.multiple_of(n * 16 + zp * 8, 8), 8)
                together = same[rows, lanes]
                mixed = (
                    jnp.where(upper, tiles[0], pltpu.roll(tiles[1], 4, 0)),
                    jnp.where(upper, pltpu.roll(tiles[0], 4, 0), tiles[1]),
                )
                for h2 in range(2):
                    h = hp * 2 + h2
                    value = mixed[h2] + chain_bias_ref[0, h] * together + mask_term[:, kt * 128 : kt * 128 + 128]
                    table[h, rows, lanes] = value * LOG2E
        return carry

    for half, group in enumerate((early, late)):
        gather_wait(2, group)
        lax.fori_loop(0, 16, functools.partial(build, half), 0)

    scale = 32 ** (-0.5) * LOG2E

    def score(i, slot):
        score_s[slot] = dot(queries[i], keys[i], 1, 1)

    def soften(slot):
        for n in range(16):
            rows = slice(n * 64, n * 64 + 64)
            scores = score_s[slot, rows] * scale + table[n // 4, n % 4 * 64 : n % 4 * 64 + 64]
            weights = jnp.exp2(scores - jnp.max(scores, axis=1, keepdims=True))
            total_s[slot, rows] = jnp.broadcast_to(1.0 / jnp.sum(weights, axis=1, keepdims=True), (64, 128))
            weight_s[slot, rows] = weights.astype(BF16)

    def attend(i, slot):
        weighted = dot(weight_s[slot], values[i]) * total_s[slot]
        total = jnp.zeros((256, 128), F32)
        for h in range(4):
            total = total + jnp.where(heads == h, weighted[h * 256 : h * 256 + 256], 0.0)
        gated_s[i] = (gates[i] * total).astype(BF16)

    def finish(part):
        rows = pl.ds(part * 4, 4)
        two = (one_mine[rows].reshape(1024, 128) + dot(gated_s[rows].reshape(1024, 128), att_out_ref[...])).astype(BF16)
        two_f = two.astype(F32)
        inner = jnp.maximum(dot(norm(two_f, 1), up_ref[...]), 0.0).astype(BF16)
        result = (two_f + dot(inner, down_ref[...])).astype(BF16).reshape(4, 16, 16, 128)
        for n in range(4):
            out_s[:, part * 4 + n] = result[n]

        def one(s, carry):
            c = lax.rem(col + s, 16)
            remote(out_s.at[c, rows], out_r.at[col, rows], 4 + part, (row, c)).start()
            return carry
        lax.fori_loop(1, 16, one, 0)
        pltpu.make_async_copy(out_s.at[col, rows], out_r.at[col, rows], local.at[4 + part]).start()

    score(0, 0)
    for i in range(8):
        if i < 7:
            score(i + 1, (i + 1) % 2)
        if i > 0:
            attend(i - 1, (i - 1) % 2)
        if i == 4:
            finish(0)
        soften(i % 2)
    attend(7, 1)
    finish(1)
    for part in range(2):
        rows = pl.ds(part * 4, 4)
        pltpu.make_async_copy(out_s.at[col, rows], out_r.at[col, rows], local.at[4 + part]).wait()
        whole = remote(out_s.at[pl.ds(0, 15), rows], out_r.at[pl.ds(0, 15), rows], 4 + part, (row, col))
        whole.wait_send()
        whole.wait_recv()

    def place_out(a, b):
        il, group, which, jl = a // 32, lax.rem(a // 8, 4), lax.rem(a // 4, 2), lax.rem(a, 4)
        return b == which * 128 + il * 16 + group * 4 + jl

    back = one_hot((256, 256), place_out)
    blocks = jnp.concatenate([out_r[2 * chip : 2 * chip + 2].reshape(256, 128) for chip in range(8)], axis=1)
    placed = dot(back, blocks).astype(BF16)
    for chip in range(8):
        out_ref[8 * chip : 8 * chip + 8] = placed[:, chip * 128 : chip * 128 + 128].reshape(8, 32, 128)


def body(pair_rep, residue_mask, chain_index, mul_in, mul_gate, mul_out, att_in, att_bias, chain_bias, att_out, trans_up, trans_down):
    vmem = pl.BlockSpec(memory_space=pltpu.VMEM)
    specs = [pl.BlockSpec(memory_space=pl.ANY)] * 12
    specs[8] = pl.BlockSpec(memory_space=pltpu.SMEM)
    sem = pltpu.SemaphoreType
    args = (
        pair_rep, residue_mask.reshape(1, -1), chain_index.reshape(1, -1), mul_in, mul_gate, mul_out, att_in, att_bias.T,
        chain_bias.reshape(1, -1), att_out, trans_up, trans_down,
    )
    return pl.pallas_call(
        kernel,
        out_shape=jax.ShapeDtypeStruct(pair_rep.shape, BF16),
        in_specs=specs,
        out_specs=vmem,
        scratch_shapes=[pltpu.VMEM(a.shape, a.dtype) for n, a in enumerate(args) if n != 8]
        + [
            pltpu.VMEM((2048, 128), F32),
            pltpu.VMEM((4096, 128), F32),
            pltpu.VMEM((128, 2, 16, 128), BF16),
            pltpu.VMEM((128, 2, 16, 128), BF16),
            pltpu.VMEM((512, 512), BF16),
            pltpu.VMEM((512, 512), BF16),
            pltpu.VMEM((2048, 128), F32),
            pltpu.VMEM((128, 16, 128), BF16),
            pltpu.VMEM((128, 16, 128), BF16),
            pltpu.VMEM((16, 4, 32, 128), BF16),
            pltpu.VMEM((8, 512, 128), BF16),
            pltpu.VMEM((4, 512, 128), BF16),
            pltpu.VMEM((4, 4, 4, 2, 8, 128), F32),
            pltpu.VMEM((4, 4, 4, 1, 8, 128), F32),
            pltpu.VMEM((4, 4, 4, 1, 8, 128), F32),
            pltpu.VMEM((4, 4, 4, 2, 8, 128), F32),
            pltpu.VMEM((4, 4, 4, 1, 8, 128), F32),
            pltpu.VMEM((4, 4, 4, 1, 8, 128), F32),
            pltpu.VMEM((4, 256, 512), F32),
            pltpu.VMEM((256, 512), F32),
            pltpu.VMEM((8, 512, 128), BF16),
            pltpu.VMEM((8, 512, 128), BF16),
            pltpu.VMEM((8, 1024, 128), BF16),
            pltpu.VMEM((8, 256, 128), F32),
            pltpu.VMEM((8, 256, 128), F32),
            pltpu.VMEM((2, 1024, 512), F32),
            pltpu.VMEM((2, 1024, 512), BF16),
            pltpu.VMEM((2, 1024, 128), F32),
            pltpu.VMEM((8, 256, 128), BF16),
            pltpu.VMEM((16, 8, 16, 128), BF16),
            pltpu.VMEM((16, 8, 16, 128), BF16),
            sem.REGULAR,
            sem.DMA((11,)),
            sem.DMA((8,)),
            sem.DMA((8,)),
            sem.DMA((8,)),
            sem.DMA((6, 3)),
            sem.DMA((6, 3)),
        ],
        compiler_params=pltpu.CompilerParams(collective_id=0, has_side_effects=True, vmem_limit_bytes=56 * 1024 * 1024),
    )(*args)


def solution(mesh):
    in_specs = (P("row", "col", None),) + (P(),) * 11
    return jax.shard_map(body, mesh=mesh, in_specs=in_specs, out_specs=P("row", "col", None), check_vma=False)
```

```python
import functools
import math

import jax
import jax.numpy as jnp
from jax import lax
from jax.experimental import pallas as pl
from jax.experimental.pallas import tpu as pltpu
from jax.sharding import PartitionSpec as P

MESH = pl.DeviceIdType.MESH
F32 = jnp.float32
BF16 = jnp.bfloat16
EPS = 1e-05
LOG2E = math.log2(math.e)
ORDERS = ((0, 1, 2), (1, 2, 0), (2, 0, 1), (1, 2, 0), (0, 1, 2), (2, 0, 1))
WHERE = {(0, 0): (0, 0), (0, 1): (0, 1), (0, 2): (1, 0), (0, 3): (2, 0), (1, 0): (3, 0), (1, 1): (3, 1), (1, 2): (4, 0), (1, 3): (5, 0)}


def norm(values, axis):
    centred = values - jnp.mean(values, axis=axis, keepdims=True)
    variance = jnp.mean(centred * centred, axis=axis, keepdims=True)
    return (centred * lax.rsqrt(variance + EPS)).astype(BF16)


def dot(a, b, ca=1, cb=0):
    return lax.dot_general(a, b, (((ca,), (cb,)), ((), ())), preferred_element_type=F32)


def one_hot(shape, hit):
    rows = lax.broadcasted_iota(jnp.int32, shape, 0)
    cols = lax.broadcasted_iota(jnp.int32, shape, 1)
    return jnp.where(hit(rows, cols), 1.0, 0.0).astype(BF16)


def kernel(
    pair_in, mask_in, chain_in, mul_in_in, mul_gate_in, mul_out_in, att_in_in, att_bias_in, chain_bias_ref,
    att_out_in, up_in, down_in, out_ref,
    pair_ref, mask_ref, chain_ref, mul_in_ref, mul_gate_ref, mul_out_ref, att_in_ref, att_bias_ref, att_out_ref, up_ref, down_ref,
    pair_f, lr_f, lr_s, lr_r, at_l, at_r, m_f, m_s, m_r, pair_rows, one_all, normed_all, bias0, bias1, bias2, bias3, bias4, bias5, table, same,
    keys, values, queries, gates, one_mine, score_s, weight_s, total_s, gated_s, out_s, out_r,
    ready, load, local, send, recv, gather_send, gather_recv,
):
    row, col = lax.axis_index("row"), lax.axis_index("col")
    me = row * 16 + col
    core = lax.rem(col, 2)
    place = (lax.rem(row, 4), col // 8 * 2 + row // 4, lax.rem(col // 2, 4))
    biases = (bias0, bias1, bias2, bias3, bias4, bias5)

    def device_at(c):
        return (lax.rem(c[1], 2) * 4 + c[0], c[1] // 2 * 8 + c[2] * 2 + core)

    def signal_row(sem):
        def one(s, carry):
            pl.semaphore_signal(sem, inc=1, device_id=(lax.rem(row + s, 8), col), device_id_type=MESH)
            return carry
        lax.fori_loop(1, 8, one, 0)

    def signal_col(sem):
        def one(s, carry):
            pl.semaphore_signal(sem, inc=1, device_id=(row, lax.rem(col + s, 16)), device_id_type=MESH)
            return carry
        lax.fori_loop(1, 16, one, 0)

    def remote(src, dst, which, target):
        return pltpu.make_async_remote_copy(src, dst, send.at[which], recv.at[which], device_id=target, device_id_type=MESH)

    loads = [
        pltpu.make_async_copy(src, dst, load.at[n])
        for n, (src, dst) in enumerate((
            (mask_in, mask_ref), (pair_in, pair_ref), (mul_in_in, mul_in_ref), (chain_in, chain_ref),
            (mul_gate_in, mul_gate_ref), (mul_out_in, mul_out_ref), (att_in_in, att_in_ref), (att_bias_in, att_bias_ref),
            (att_out_in, att_out_ref), (up_in, up_ref), (down_in, down_ref),
        ))
    ]
    for one in loads[:3]:
        one.start()
    barrier = pltpu.get_barrier_semaphore()
    signal_row(barrier)
    signal_col(barrier)
    for one in loads[3:]:
        one.start()
    loads[0].wait()

    def send_pair(part):
        rows = pl.ds(2 * part, 2)

        def one(s, carry):
            c = lax.rem(col + s, 16)
            remote(pair_ref.at[pl.ds(4 * c + 2 * part, 2)], pair_rows.at[col, rows], 6 + part, (row, c)).start()
            return carry
        lax.fori_loop(1, 16, one, 0)
        pltpu.make_async_copy(pair_ref.at[pl.ds(4 * col + 2 * part, 2)], pair_rows.at[col, rows], local.at[6 + part]).start()

    mask = mask_ref[...].astype(F32)
    pick_rows = one_hot((512, 128), lambda a, b: a == row * 64 + lax.rem(b, 64))
    row_mask = dot(jnp.broadcast_to(mask, (16, 512)).astype(BF16), pick_rows)
    place_col = lax.broadcasted_iota(jnp.int32, (16, 512), 1) - (col * 32 + 2 * lax.broadcasted_iota(jnp.int32, (16, 512), 0))
    even = jnp.sum(jnp.where(place_col == 0, mask, 0.0), axis=1, keepdims=True)
    odd = jnp.sum(jnp.where(place_col == 1, mask, 0.0), axis=1, keepdims=True)
    lanes16 = lax.broadcasted_iota(jnp.int32, (16, 128), 1)
    pair_mask = jnp.where(lanes16 < 64, even, odd) * row_mask
    loads[1].wait()
    loads[2].wait()
    pair_f[...] = pair_ref[...].astype(F32).reshape(2048, 128)
    mul_in_t = mul_in_ref[...].T
    for step in range(2):
        if step == 1:
            pl.semaphore_wait(barrier, 22)
            for s in range(1, 8):
                pl.semaphore_signal(ready.at[s], inc=1, device_id=(lax.rem(row + s, 8), col), device_id_type=MESH)
            send_pair(0)
        parts = [pair_f[pl.ds(16 * step + u, 64, stride=32), :] for u in range(16)]
        normed = norm(jnp.concatenate(parts, axis=0).T, 0)
        projected = dot(mul_in_t, normed)
        masks = jnp.concatenate([pair_mask[8 * step + v : 8 * step + v + 1] for v in range(8)], axis=1)
        left = masks * jax.nn.sigmoid(projected[128:256]) * projected[:128]
        right = masks * jax.nn.sigmoid(projected[384:]) * projected[256:384]
        for v in range(8):
            lr_f[pl.ds(8 * step + v, 128, stride=32), :] = left[:, v * 128 : v * 128 + 128]
            lr_f[pl.ds(16 + 8 * step + v, 128, stride=32), :] = right[:, v * 128 : v * 128 + 128]
    lr_s[...] = lr_f[...].reshape(128, 2, 16, 128).astype(BF16)

    for one in loads[3:]:
        one.wait()

    def to_row(src, dst, which, s):
        r = lax.rem(row + s, 8)

        def one(n, carry):
            c = lax.rem(col + n, 16)
            remote(src.at[r * 16 + c], dst.at[me], which, (r, c)).start()
            return carry
        lax.fori_loop(1 if s == 0 else 0, 16, one, 0)

    def to_all(src, dst, which):
        for s in range(8):
            if s > 0 and which == 0:
                pl.semaphore_wait(ready.at[8 - s], 1)
            to_row(src, dst, which, s)
        pltpu.make_async_copy(src.at[me], dst.at[me], local.at[which]).start()

    def all_here(src, dst, which):
        pltpu.make_async_copy(src.at[me], dst.at[me], local.at[which]).wait()
        whole = remote(src.at[pl.ds(0, 127)], dst.at[pl.ds(0, 127)], which, (row, col))
        whole.wait_send()
        whole.wait_recv()

    to_all(lr_s, lr_r, 0)

    def place_left(a, b):
        k, il, r, g = b // 128, lax.rem(b // 32, 4), lax.rem(b // 16, 2), lax.rem(b, 16)
        return a == r * 128 + k * 64 + 4 * g + il

    def place_right(a, b):
        k, r, i = b // 128, lax.rem(b // 64, 2), lax.rem(b, 64)
        return a == r * 128 + k * 64 + i

    orders = (one_hot((256, 256), place_left), one_hot((256, 256), place_right))
    head_rows = lax.broadcasted_iota(jnp.int32, (16, 512), 0)
    chains = jnp.where(head_rows == chain_ref[...], 1.0, 0.0).astype(BF16)
    mine = one_hot((256, 512), lambda a, b: b == a // 4 * 8 + core * 4 + lax.rem(a, 4))
    chains_mine = dot(chains, mine, 1, 1).astype(BF16)
    same[...] = dot(chains_mine.T, chains)

    all_here(lr_s, lr_r, 0)

    send_pair(1)
    for side, at in ((0, at_l), (1, at_r)):
        here = [
            jnp.concatenate([lr_r[(2 * rp + o) * 16 : (2 * rp + o + 1) * 16, side].reshape(256, 128) for o in range(2)], axis=1)
            for rp in range(4)
        ]
        turned = dot(jnp.concatenate(here, axis=0), orders[side]).astype(BF16)
        for rp in range(4):
            for k in range(2):
                at[k * 256 : k * 256 + 256, rp * 128 : rp * 128 + 128] = turned[rp * 256 : rp * 256 + 256, k * 128 : k * 128 + 128]
    product = dot(at_l[...], at_r[...], 0, 0)
    for rp in range(4):
        for il in range(4):
            at = rp * 128 + il * 32
            for jt in range(4):
                m_f[pl.ds(rp * 512 + il * 4 + jt, 32, stride=16), :] = product[at : at + 32, jt * 128 : jt * 128 + 128]
    m_s[...] = m_f[...].reshape(128, 16, 128).astype(BF16)
    to_all(m_s, m_r, 2)

    for part in range(2):
        rows = pl.ds(2 * part, 2)
        pltpu.make_async_copy(pair_ref.at[pl.ds(0, 2)], pair_rows.at[0, rows], local.at[6 + part]).wait()
        whole = remote(pair_rows.at[pl.ds(0, 15), rows], pair_rows.at[pl.ds(0, 15), rows], 6 + part, (row, col))
        whole.wait_send()
        whole.wait_recv()

    def pair_block(half):
        blocks = [pair_rows[8 * half : 8 * half + 8, il].reshape(256, 128) for il in range(4)]
        return jnp.concatenate(blocks, axis=0).astype(F32)

    for half in range(2):
        pair_f[half * 1024 : half * 1024 + 1024] = jax.nn.sigmoid(dot(norm(pair_block(half), 1), mul_gate_ref[...]))
    all_here(m_s, m_r, 2)

    early, late = (0, 1, 2), (3, 4, 5)

    def plane_start(which):
        def one(n, carry):
            for o in which:
                a, b, c = ORDERS[o]
                there = list(place)
                there[a] = lax.rem(place[a] + lax.rem(n, 4), 4)
                there[b] = lax.rem(place[b] + n // 4, 4)
                ref = biases[o].at[place[c], place[b], place[a]]
                pltpu.make_async_remote_copy(
                    ref, ref, gather_send.at[o, 0], gather_recv.at[o, 0], device_id=device_at(there), device_id_type=MESH
                ).start()
            return carry
        lax.fori_loop(1, 16, one, 0)

    def plane_wait(which):
        for o in which:
            ref = m_f.at[pl.ds(0, 120 * biases[o].shape[3])]
            whole = pltpu.make_async_remote_copy(
                ref, ref, gather_send.at[o, 0], gather_recv.at[o, 0], device_id=(row, col), device_id_type=MESH
            )
            whole.wait_send()
            whole.wait_recv()

    def axis_start(which):
        for s in (1, 3, 2):
            for o in which:
                c = ORDERS[o][2]
                there = list(place)
                there[c] = lax.rem(place[c] + s, 4)
                ref = biases[o].at[place[c]]
                pltpu.make_async_remote_copy(
                    ref, ref, gather_send.at[o, 1], gather_recv.at[o, 1], device_id=device_at(there), device_id_type=MESH
                ).start()

    def axis_wait(which):
        for o in which:
            ref = biases[o].at[pl.ds(0, 3)]
            whole = pltpu.make_async_remote_copy(
                ref, ref, gather_send.at[o, 1], gather_recv.at[o, 1], device_id=(row, col), device_id_type=MESH
            )
            whole.wait_send()
            whole.wait_recv()

    m_f[...] = m_r[...].astype(F32).reshape(2048, 128)
    bias_in = jnp.concatenate([att_bias_ref[...].astype(F32), jnp.zeros((4, 128), F32)], axis=0).astype(BF16)
    for half in range(2):
        tiles = [m_f[pl.ds(il * 4 + 2 * half + t, 128, stride=16), :] for il in range(4) for t in range(2)]
        update = dot(norm(jnp.concatenate(tiles, axis=1), 0), mul_out_ref[...], 0, 0)
        one = (pair_block(half) + pair_f[half * 1024 : half * 1024 + 1024] * update).astype(BF16)
        normed = norm(one.astype(F32), 1)
        bias = dot(bias_in, normed, 1, 1)
        for il in range(4):
            one_all[core * 4 + il, half * 256 : half * 256 + 256] = one[il * 256 : il * 256 + 256]
            normed_all[il, half * 256 : half * 256 + 256] = normed[il * 256 : il * 256 + 256]
            for t in range(2):
                lanes = slice((il * 2 + t) * 128, (il * 2 + t) * 128 + 128)
                for h in range(4):
                    o, slot = WHERE[h // 2, 2 * half + t]
                    a, b, c = (place[axis] for axis in ORDERS[o])
                    biases[o][c, b, a, slot, h % 2 * 4 + il : h % 2 * 4 + il + 1, :] = bias[h : h + 1, lanes]
    plane_start(early)
    plane_start(late)
    sibling = (row, col + 1 - 2 * core)
    swap = remote(one_all.at[pl.ds(core * 4, 4)], one_all.at[pl.ds(core * 4, 4)], 3, sibling)
    swap.start()

    heads = lax.broadcasted_iota(jnp.int32, (256, 128), 1) // 32

    def project(first, normed):
        four = pl.ds(first, 4)
        kv = dot(normed, att_in_ref[:, 128:384]).astype(BF16)
        keys[four] = kv[:, :128].reshape(4, 512, 128)
        values[four] = kv[:, 128:].reshape(4, 512, 128)
        picked = []
        for n in range(4):
            both = dot(mine, jnp.concatenate([normed[n * 512 : n * 512 + 512], one_all[first + n]], axis=1))
            picked.append(both[:, :128].astype(BF16))
            one_mine[first + n] = both[:, 128:]
        picked = jnp.concatenate(picked, axis=0)
        query = dot(picked, att_in_ref[:, :128])
        for n in range(4):
            for h in range(4):
                queries[first + n, h * 256 : h * 256 + 256] = jnp.where(heads == h, query[n * 256 : n * 256 + 256], 0.0).astype(BF16)
        gates[four] = jax.nn.sigmoid(dot(picked, att_in_ref[:, 384:])).reshape(4, 256, 128)

    plane_wait(early)
    axis_start(early)
    project(core * 4, normed_all[...].reshape(2048, 128))
    plane_wait(late)
    axis_start(late)
    swap.wait()
    other = 4 - core * 4
    project(other, norm(one_all[pl.ds(other, 4)].reshape(2048, 128).astype(F32), 1))

    mask_term = 1000000000.0 * (mask - 1.0)
    upper = lax.broadcasted_iota(jnp.int32, (8, 128), 0) < 4

    def build(hp, n, carry):
        x, y = lax.rem(n // 2, 4), lax.rem(n, 2) * 2 + n // 8
        for kt in range(4):
            o, slot = WHERE[hp, kt]
            lanes = pl.ds(kt * 128, 128)
            for zp in range(2):
                tiles = []
                for z in (2 * zp, 2 * zp + 1):
                    at = (x, y, z)
                    a, b, c = (at[axis] for axis in ORDERS[o])
                    tiles.append(biases[o][c, b, a, slot])
                rows = pl.ds(pl.multiple_of(n * 16 + zp * 8, 8), 8)
                together = same[rows, lanes]
                mixed = (
                    jnp.where(upper, tiles[0], pltpu.roll(tiles[1], 4, 0)),
                    jnp.where(upper, pltpu.roll(tiles[0], 4, 0), tiles[1]),
                )
                for h2 in range(2):
                    h = hp * 2 + h2
                    value = mixed[h2] + chain_bias_ref[0, h] * together + mask_term[:, kt * 128 : kt * 128 + 128]
                    table[h, rows, lanes] = value * LOG2E
        return carry

    scale = 32 ** (-0.5) * LOG2E

    def score(hp, i, slot):
        score_s[slot] = dot(queries[i, hp * 512 : hp * 512 + 512], keys[i], 1, 1)

    def soften(hp, slot):
        for n in range(8):
            rows = slice(n * 64, n * 64 + 64)
            scores = score_s[slot, rows] * scale + table[2 * hp + n // 4, n % 4 * 64 : n % 4 * 64 + 64]
            weights = jnp.exp2(scores - jnp.max(scores, axis=1, keepdims=True))
            total_s[slot, rows] = jnp.broadcast_to(1.0 / jnp.sum(weights, axis=1, keepdims=True), (64, 128))
            weight_s[slot, rows] = weights.astype(BF16)

    def attend(hp, i, slot):
        weighted = dot(weight_s[slot], values[i]) * total_s[slot]
        total = jnp.where(heads == 2 * hp, weighted[:256], jnp.where(heads == 2 * hp + 1, weighted[256:], 0.0))
        gated = (gates[i] * total).astype(BF16)
        gated_s[i] = gated if hp == 0 else jnp.where(heads < 2, gated_s[i], gated)

    def finish(part):
        rows = pl.ds(part * 4, 4)
        two = (one_mine[rows].reshape(1024, 128) + dot(gated_s[rows].reshape(1024, 128), att_out_ref[...])).astype(BF16)
        two_f = two.astype(F32)
        inner = jnp.maximum(dot(norm(two_f, 1), up_ref[...]), 0.0).astype(BF16)
        result = (two_f + dot(inner, down_ref[...])).astype(BF16).reshape(4, 16, 16, 128)
        for n in range(4):
            out_s[:, part * 4 + n] = result[n]

    def send_out(part):
        rows = pl.ds(part * 4, 4)

        def one(s, carry):
            c = lax.rem(col + s, 16)
            remote(out_s.at[c, rows], out_r.at[col, rows], 4 + part, (row, c)).start()
            return carry
        lax.fori_loop(1, 16, one, 0)
        pltpu.make_async_copy(out_s.at[col, rows], out_r.at[col, rows], local.at[4 + part]).start()

    for hp, group in enumerate((early, late)):
        score(hp, 0, 0)
        axis_wait(group)
        lax.fori_loop(0, 16, functools.partial(build, hp), 0)
        for i in range(8):
            if i < 7:
                score(hp, i + 1, (i + 1) % 2)
            if i > 0:
                attend(hp, i - 1, (i - 1) % 2)
            if hp == 1 and i == 4:
                finish(0)
            soften(hp, i % 2)
            if hp == 1 and i == 4:
                send_out(0)
        attend(hp, 7, 1)
    finish(1)
    send_out(1)
    for part in range(2):
        rows = pl.ds(part * 4, 4)
        pltpu.make_async_copy(out_s.at[col, rows], out_r.at[col, rows], local.at[4 + part]).wait()
        whole = remote(out_s.at[pl.ds(0, 15), rows], out_r.at[pl.ds(0, 15), rows], 4 + part, (row, col))
        whole.wait_send()
        whole.wait_recv()

    def place_out(a, b):
        il, group, which, jl = a // 32, lax.rem(a // 8, 4), lax.rem(a // 4, 2), lax.rem(a, 4)
        return b == which * 128 + il * 16 + group * 4 + jl

    back = one_hot((256, 256), place_out)
    blocks = jnp.concatenate([out_r[2 * chip : 2 * chip + 2].reshape(256, 128) for chip in range(8)], axis=1)
    placed = dot(back, blocks).astype(BF16)
    for chip in range(8):
        out_ref[8 * chip : 8 * chip + 8] = placed[:, chip * 128 : chip * 128 + 128].reshape(8, 32, 128)


def body(pair_rep, residue_mask, chain_index, mul_in, mul_gate, mul_out, att_in, att_bias, chain_bias, att_out, trans_up, trans_down):
    vmem = pl.BlockSpec(memory_space=pltpu.VMEM)
    specs = [pl.BlockSpec(memory_space=pl.ANY)] * 12
    specs[8] = pl.BlockSpec(memory_space=pltpu.SMEM)
    sem = pltpu.SemaphoreType
    args = (
        pair_rep, residue_mask.reshape(1, -1), chain_index.reshape(1, -1), mul_in, mul_gate, mul_out, att_in, att_bias.T,
        chain_bias.reshape(1, -1), att_out, trans_up, trans_down,
    )
    return pl.pallas_call(
        kernel,
        out_shape=jax.ShapeDtypeStruct(pair_rep.shape, BF16),
        in_specs=specs,
        out_specs=vmem,
        scratch_shapes=[pltpu.VMEM(a.shape, a.dtype) for n, a in enumerate(args) if n != 8]
        + [
            pltpu.VMEM((2048, 128), F32),
            pltpu.VMEM((4096, 128), F32),
            pltpu.VMEM((128, 2, 16, 128), BF16),
            pltpu.VMEM((128, 2, 16, 128), BF16),
            pltpu.VMEM((512, 512), BF16),
            pltpu.VMEM((512, 512), BF16),
            pltpu.VMEM((2048, 128), F32),
            pltpu.VMEM((128, 16, 128), BF16),
            pltpu.VMEM((128, 16, 128), BF16),
            pltpu.VMEM((16, 4, 32, 128), BF16),
            pltpu.VMEM((8, 512, 128), BF16),
            pltpu.VMEM((4, 512, 128), BF16),
            pltpu.VMEM((4, 4, 4, 2, 8, 128), F32),
            pltpu.VMEM((4, 4, 4, 1, 8, 128), F32),
            pltpu.VMEM((4, 4, 4, 1, 8, 128), F32),
            pltpu.VMEM((4, 4, 4, 2, 8, 128), F32),
            pltpu.VMEM((4, 4, 4, 1, 8, 128), F32),
            pltpu.VMEM((4, 4, 4, 1, 8, 128), F32),
            pltpu.VMEM((4, 256, 512), F32),
            pltpu.VMEM((256, 512), F32),
            pltpu.VMEM((8, 512, 128), BF16),
            pltpu.VMEM((8, 512, 128), BF16),
            pltpu.VMEM((8, 1024, 128), BF16),
            pltpu.VMEM((8, 256, 128), F32),
            pltpu.VMEM((8, 256, 128), F32),
            pltpu.VMEM((2, 512, 512), F32),
            pltpu.VMEM((2, 512, 512), BF16),
            pltpu.VMEM((2, 512, 128), F32),
            pltpu.VMEM((8, 256, 128), BF16),
            pltpu.VMEM((16, 8, 16, 128), BF16),
            pltpu.VMEM((16, 8, 16, 128), BF16),
            sem.REGULAR((8,)),
            sem.DMA((11,)),
            sem.DMA((8,)),
            sem.DMA((8,)),
            sem.DMA((8,)),
            sem.DMA((6, 2)),
            sem.DMA((6, 2)),
        ],
        compiler_params=pltpu.CompilerParams(collective_id=0, has_side_effects=True, vmem_limit_bytes=56 * 1024 * 1024),
    )(*args)


def solution(mesh):
    in_specs = (P("row", "col", None),) + (P(),) * 11
    return jax.shard_map(body, mesh=mesh, in_specs=in_specs, out_specs=P("row", "col", None), check_vma=False)
```

```python
import functools
import math

import jax
import jax.numpy as jnp
from jax import lax
from jax.experimental import pallas as pl
from jax.experimental.pallas import tpu as pltpu
from jax.sharding import PartitionSpec as P

MESH = pl.DeviceIdType.MESH
F32 = jnp.float32
BF16 = jnp.bfloat16
EPS = 1e-05
LOG2E = math.log2(math.e)
ORDERS = ((0, 1, 2), (1, 2, 0), (2, 0, 1), (1, 2, 0), (0, 1, 2), (2, 0, 1))
WHERE = {(0, 0): (0, 0), (0, 1): (0, 1), (0, 2): (1, 0), (0, 3): (2, 0), (1, 0): (3, 0), (1, 1): (3, 1), (1, 2): (4, 0), (1, 3): (5, 0)}


def norm(values, axis):
    centred = values - jnp.mean(values, axis=axis, keepdims=True)
    variance = jnp.mean(centred * centred, axis=axis, keepdims=True)
    return (centred * lax.rsqrt(variance + EPS)).astype(BF16)


def dot(a, b, ca=1, cb=0):
    return lax.dot_general(a, b, (((ca,), (cb,)), ((), ())), preferred_element_type=F32)


def one_hot(shape, hit):
    rows = lax.broadcasted_iota(jnp.int32, shape, 0)
    cols = lax.broadcasted_iota(jnp.int32, shape, 1)
    return jnp.where(hit(rows, cols), 1.0, 0.0).astype(BF16)


def kernel(
    pair_in, mask_in, chain_in, mul_in_in, mul_gate_in, mul_out_in, att_in_in, att_bias_in, chain_bias_ref,
    att_out_in, up_in, down_in, out_ref,
    pair_ref, mask_ref, chain_ref, mul_in_ref, mul_gate_ref, mul_out_ref, att_in_ref, att_bias_ref, att_out_ref, up_ref, down_ref,
    pair_f, lr_f, lr_s, lr_r, at_l, at_r, m_f, m_s, m_r, pair_rows, one_all, normed_all, bias0, bias1, bias2, bias3, bias4, bias5, table, same,
    keys, values, queries, gates, one_mine, score_s, weight_s, gated_s, out_s, out_r,
    ready, load, local, send, recv, gather_send, gather_recv,
):
    row, col = lax.axis_index("row"), lax.axis_index("col")
    me = row * 16 + col
    core = lax.rem(col, 2)
    place = (lax.rem(row, 4), col // 8 * 2 + row // 4, lax.rem(col // 2, 4))
    biases = (bias0, bias1, bias2, bias3, bias4, bias5)

    def device_at(c):
        return (lax.rem(c[1], 2) * 4 + c[0], c[1] // 2 * 8 + c[2] * 2 + core)

    def signal_row(sem):
        def one(s, carry):
            pl.semaphore_signal(sem, inc=1, device_id=(lax.rem(row + s, 8), col), device_id_type=MESH)
            return carry
        lax.fori_loop(1, 8, one, 0)

    def signal_col(sem):
        def one(s, carry):
            pl.semaphore_signal(sem, inc=1, device_id=(row, lax.rem(col + s, 16)), device_id_type=MESH)
            return carry
        lax.fori_loop(1, 16, one, 0)

    def remote(src, dst, which, target):
        return pltpu.make_async_remote_copy(src, dst, send.at[which], recv.at[which], device_id=target, device_id_type=MESH)

    loads = [
        pltpu.make_async_copy(src, dst, load.at[n])
        for n, (src, dst) in enumerate((
            (mask_in, mask_ref), (pair_in, pair_ref), (mul_in_in, mul_in_ref), (chain_in, chain_ref),
            (mul_gate_in, mul_gate_ref), (mul_out_in, mul_out_ref), (att_in_in, att_in_ref), (att_bias_in, att_bias_ref),
            (att_out_in, att_out_ref), (up_in, up_ref), (down_in, down_ref),
        ))
    ]
    for one in loads[:3]:
        one.start()
    barrier = pltpu.get_barrier_semaphore()
    signal_row(barrier)
    signal_col(barrier)
    for one in loads[3:]:
        one.start()
    loads[0].wait()

    def send_pair(part):
        rows = pl.ds(2 * part, 2)

        def one(s, carry):
            c = lax.rem(col + s, 16)
            remote(pair_ref.at[pl.ds(4 * c + 2 * part, 2)], pair_rows.at[col, rows], 6 + part, (row, c)).start()
            return carry
        lax.fori_loop(1, 16, one, 0)
        pltpu.make_async_copy(pair_ref.at[pl.ds(4 * col + 2 * part, 2)], pair_rows.at[col, rows], local.at[6 + part]).start()

    mask = mask_ref[...].astype(F32)
    pick_rows = one_hot((512, 128), lambda a, b: a == row * 64 + lax.rem(b, 64))
    row_mask = dot(jnp.broadcast_to(mask, (16, 512)).astype(BF16), pick_rows)
    place_col = lax.broadcasted_iota(jnp.int32, (16, 512), 1) - (col * 32 + 2 * lax.broadcasted_iota(jnp.int32, (16, 512), 0))
    even = jnp.sum(jnp.where(place_col == 0, mask, 0.0), axis=1, keepdims=True)
    odd = jnp.sum(jnp.where(place_col == 1, mask, 0.0), axis=1, keepdims=True)
    lanes16 = lax.broadcasted_iota(jnp.int32, (16, 128), 1)
    pair_mask = jnp.where(lanes16 < 64, even, odd) * row_mask
    loads[1].wait()
    loads[2].wait()
    pair_f[...] = pair_ref[...].astype(F32).reshape(2048, 128)
    mul_in_t = mul_in_ref[...].T
    for step in range(2):
        if step == 1:
            pl.semaphore_wait(barrier, 22)
            for s in range(1, 8):
                pl.semaphore_signal(ready.at[s], inc=1, device_id=(lax.rem(row + s, 8), col), device_id_type=MESH)
            send_pair(0)
        parts = [pair_f[pl.ds(16 * step + u, 64, stride=32), :] for u in range(16)]
        normed = norm(jnp.concatenate(parts, axis=0).T, 0)
        projected = dot(mul_in_t, normed)
        masks = jnp.concatenate([pair_mask[8 * step + v : 8 * step + v + 1] for v in range(8)], axis=1)
        left = masks * jax.nn.sigmoid(projected[128:256]) * projected[:128]
        right = masks * jax.nn.sigmoid(projected[384:]) * projected[256:384]
        for v in range(8):
            lr_f[pl.ds(8 * step + v, 128, stride=32), :] = left[:, v * 128 : v * 128 + 128]
            lr_f[pl.ds(16 + 8 * step + v, 128, stride=32), :] = right[:, v * 128 : v * 128 + 128]
    lr_s[...] = lr_f[...].reshape(128, 2, 16, 128).astype(BF16)

    for one in loads[3:]:
        one.wait()

    def to_row(src, dst, which, s):
        r = lax.rem(row + s, 8)

        def one(n, carry):
            c = lax.rem(col + n, 16)
            remote(src.at[r * 16 + c], dst.at[me], which, (r, c)).start()
            return carry
        lax.fori_loop(1 if s == 0 else 0, 16, one, 0)

    def to_all(src, dst, which):
        for s in range(8):
            if s > 0 and which == 0:
                pl.semaphore_wait(ready.at[8 - s], 1)
            to_row(src, dst, which, s)
        pltpu.make_async_copy(src.at[me], dst.at[me], local.at[which]).start()

    def all_here(src, dst, which):
        pltpu.make_async_copy(src.at[me], dst.at[me], local.at[which]).wait()
        whole = remote(src.at[pl.ds(0, 127)], dst.at[pl.ds(0, 127)], which, (row, col))
        whole.wait_send()
        whole.wait_recv()

    to_all(lr_s, lr_r, 0)

    def place_left(a, b):
        k, il, r, g = b // 128, lax.rem(b // 32, 4), lax.rem(b // 16, 2), lax.rem(b, 16)
        return a == r * 128 + k * 64 + 4 * g + il

    def place_right(a, b):
        k, r, i = b // 128, lax.rem(b // 64, 2), lax.rem(b, 64)
        return a == r * 128 + k * 64 + i

    orders = (one_hot((256, 256), place_left), one_hot((256, 256), place_right))
    head_rows = lax.broadcasted_iota(jnp.int32, (16, 512), 0)
    chains = jnp.where(head_rows == chain_ref[...], 1.0, 0.0).astype(BF16)
    mine = one_hot((256, 512), lambda a, b: b == a // 4 * 8 + core * 4 + lax.rem(a, 4))
    chains_mine = dot(chains, mine, 1, 1).astype(BF16)
    same[...] = dot(chains_mine.T, chains)

    all_here(lr_s, lr_r, 0)

    send_pair(1)
    for side, at in ((0, at_l), (1, at_r)):
        here = [
            jnp.concatenate([lr_r[(2 * rp + o) * 16 : (2 * rp + o + 1) * 16, side].reshape(256, 128) for o in range(2)], axis=1)
            for rp in range(4)
        ]
        turned = dot(jnp.concatenate(here, axis=0), orders[side]).astype(BF16)
        for rp in range(4):
            for k in range(2):
                at[k * 256 : k * 256 + 256, rp * 128 : rp * 128 + 128] = turned[rp * 256 : rp * 256 + 256, k * 128 : k * 128 + 128]
    product = dot(at_l[...], at_r[...], 0, 0)
    for rp in range(4):
        for il in range(4):
            at = rp * 128 + il * 32
            for jt in range(4):
                m_f[pl.ds(rp * 512 + il * 4 + jt, 32, stride=16), :] = product[at : at + 32, jt * 128 : jt * 128 + 128]
    m_s[...] = m_f[...].reshape(128, 16, 128).astype(BF16)
    to_all(m_s, m_r, 2)

    for part in range(2):
        rows = pl.ds(2 * part, 2)
        pltpu.make_async_copy(pair_ref.at[pl.ds(0, 2)], pair_rows.at[0, rows], local.at[6 + part]).wait()
        whole = remote(pair_rows.at[pl.ds(0, 15), rows], pair_rows.at[pl.ds(0, 15), rows], 6 + part, (row, col))
        whole.wait_send()
        whole.wait_recv()

    def pair_block(half):
        blocks = [pair_rows[8 * half : 8 * half + 8, il].reshape(256, 128) for il in range(4)]
        return jnp.concatenate(blocks, axis=0).astype(F32)

    for half in range(2):
        pair_f[half * 1024 : half * 1024 + 1024] = jax.nn.sigmoid(dot(norm(pair_block(half), 1), mul_gate_ref[...]))
    all_here(m_s, m_r, 2)

    early, late = (0, 1, 2), (3, 4, 5)

    def plane_start(which):
        def one(n, carry):
            for o in which:
                a, b, c = ORDERS[o]
                there = list(place)
                there[a] = lax.rem(place[a] + lax.rem(n, 4), 4)
                there[b] = lax.rem(place[b] + n // 4, 4)
                ref = biases[o].at[place[c], place[b], place[a]]
                pltpu.make_async_remote_copy(
                    ref, ref, gather_send.at[o, 0], gather_recv.at[o, 0], device_id=device_at(there), device_id_type=MESH
                ).start()
            return carry
        lax.fori_loop(1, 16, one, 0)

    def plane_wait(which):
        for o in which:
            ref = m_f.at[pl.ds(0, 120 * biases[o].shape[3])]
            whole = pltpu.make_async_remote_copy(
                ref, ref, gather_send.at[o, 0], gather_recv.at[o, 0], device_id=(row, col), device_id_type=MESH
            )
            whole.wait_send()
            whole.wait_recv()

    def axis_start(which):
        for s in (1, 3, 2):
            for o in which:
                c = ORDERS[o][2]
                there = list(place)
                there[c] = lax.rem(place[c] + s, 4)
                ref = biases[o].at[place[c]]
                pltpu.make_async_remote_copy(
                    ref, ref, gather_send.at[o, 1], gather_recv.at[o, 1], device_id=device_at(there), device_id_type=MESH
                ).start()

    def axis_wait(which):
        for o in which:
            ref = biases[o].at[pl.ds(0, 3)]
            whole = pltpu.make_async_remote_copy(
                ref, ref, gather_send.at[o, 1], gather_recv.at[o, 1], device_id=(row, col), device_id_type=MESH
            )
            whole.wait_send()
            whole.wait_recv()

    m_f[...] = m_r[...].astype(F32).reshape(2048, 128)
    bias_in = jnp.concatenate([att_bias_ref[...].astype(F32), jnp.zeros((4, 128), F32)], axis=0).astype(BF16)
    for half in range(2):
        tiles = [m_f[pl.ds(il * 4 + 2 * half + t, 128, stride=16), :] for il in range(4) for t in range(2)]
        update = dot(norm(jnp.concatenate(tiles, axis=1), 0), mul_out_ref[...], 0, 0)
        one = (pair_block(half) + pair_f[half * 1024 : half * 1024 + 1024] * update).astype(BF16)
        normed = norm(one.astype(F32), 1)
        bias = dot(bias_in, normed, 1, 1)
        for il in range(4):
            one_all[core * 4 + il, half * 256 : half * 256 + 256] = one[il * 256 : il * 256 + 256]
            normed_all[il, half * 256 : half * 256 + 256] = normed[il * 256 : il * 256 + 256]
            for t in range(2):
                lanes = slice((il * 2 + t) * 128, (il * 2 + t) * 128 + 128)
                for h in range(4):
                    o, slot = WHERE[h // 2, 2 * half + t]
                    a, b, c = (place[axis] for axis in ORDERS[o])
                    biases[o][c, b, a, slot, h % 2 * 4 + il : h % 2 * 4 + il + 1, :] = bias[h : h + 1, lanes]
    plane_start(early)
    plane_start(late)
    sibling = (row, col + 1 - 2 * core)
    swap = remote(one_all.at[pl.ds(core * 4, 4)], one_all.at[pl.ds(core * 4, 4)], 3, sibling)
    swap.start()

    heads = lax.broadcasted_iota(jnp.int32, (256, 128), 1) // 32

    scale = 32 ** (-0.5) * LOG2E

    def project(first, normed):
        four = pl.ds(first, 4)
        kv = dot(normed, att_in_ref[:, 128:384]).astype(BF16)
        keys[four] = kv[:, :128].reshape(4, 512, 128)
        values[four, :, 0:128] = kv[:, 128:].reshape(4, 512, 128)
        values[four, :, 128:256] = jnp.ones((4, 512, 128), BF16)
        picked = []
        for n in range(4):
            both = dot(mine, jnp.concatenate([normed[n * 512 : n * 512 + 512], one_all[first + n]], axis=1))
            picked.append(both[:, :128].astype(BF16))
            one_mine[first + n] = both[:, 128:]
        picked = jnp.concatenate(picked, axis=0)
        query = dot(picked, att_in_ref[:, :128]) * scale
        for n in range(4):
            for h in range(4):
                queries[first + n, h * 256 : h * 256 + 256] = jnp.where(heads == h, query[n * 256 : n * 256 + 256], 0.0).astype(BF16)
        gates[four] = jax.nn.sigmoid(dot(picked, att_in_ref[:, 384:])).reshape(4, 256, 128)

    plane_wait(early)
    axis_start(early)
    project(core * 4, normed_all[...].reshape(2048, 128))
    plane_wait(late)
    axis_start(late)
    swap.wait()
    other = 4 - core * 4
    project(other, norm(one_all[pl.ds(other, 4)].reshape(2048, 128).astype(F32), 1))

    mask_term = 1000000000.0 * (mask - 1.0)
    upper = lax.broadcasted_iota(jnp.int32, (8, 128), 0) < 4

    def build(hp, n, carry):
        x, y = lax.rem(n // 2, 4), lax.rem(n, 2) * 2 + n // 8
        for kt in range(4):
            o, slot = WHERE[hp, kt]
            lanes = pl.ds(kt * 128, 128)
            for zp in range(2):
                tiles = []
                for z in (2 * zp, 2 * zp + 1):
                    at = (x, y, z)
                    a, b, c = (at[axis] for axis in ORDERS[o])
                    tiles.append(biases[o][c, b, a, slot])
                rows = pl.ds(pl.multiple_of(n * 16 + zp * 8, 8), 8)
                together = same[rows, lanes]
                mixed = (
                    jnp.where(upper, tiles[0], pltpu.roll(tiles[1], 4, 0)),
                    jnp.where(upper, pltpu.roll(tiles[0], 4, 0), tiles[1]),
                )
                for h2 in range(2):
                    h = hp * 2 + h2
                    value = mixed[h2] + chain_bias_ref[0, h] * together + mask_term[:, kt * 128 : kt * 128 + 128]
                    table[h, rows, lanes] = value * LOG2E
        return carry


    def score(hp, i):
        score_s[hp, i] = dot(queries[i, hp * 512 : hp * 512 + 512], keys[i], 1, 1)

    def soften(hp, i, slot):
        for n in range(8):
            rows = slice(n * 64, n * 64 + 64)
            scores = score_s[hp, i, rows] + table[2 * hp + n // 4, n % 4 * 64 : n % 4 * 64 + 64]
            weights = jnp.exp2(scores - jnp.max(scores, axis=1, keepdims=True))
            weight_s[slot, rows] = weights.astype(BF16)

    def attend(hp, i, slot):
        weighted = dot(weight_s[slot], values[i])
        weighted = weighted[:, :128] / weighted[:, 128:]
        total = jnp.where(heads == 2 * hp, weighted[:256], jnp.where(heads == 2 * hp + 1, weighted[256:], 0.0))
        gated = (gates[i] * total).astype(BF16)
        gated_s[i] = gated if hp == 0 else jnp.where(heads < 2, gated_s[i], gated)

    def finish(part):
        rows = pl.ds(part * 4, 4)
        two = (one_mine[rows].reshape(1024, 128) + dot(gated_s[rows].reshape(1024, 128), att_out_ref[...])).astype(BF16)
        two_f = two.astype(F32)
        inner = jnp.maximum(dot(norm(two_f, 1), up_ref[...]), 0.0).astype(BF16)
        result = (two_f + dot(inner, down_ref[...])).astype(BF16).reshape(4, 16, 16, 128)
        for n in range(4):
            out_s[:, part * 4 + n] = result[n]

    def send_out(part):
        rows = pl.ds(part * 4, 4)

        def one(s, carry):
            c = lax.rem(col + s, 16)
            remote(out_s.at[c, rows], out_r.at[col, rows], 4 + part, (row, c)).start()
            return carry
        lax.fori_loop(1, 16, one, 0)
        pltpu.make_async_copy(out_s.at[col, rows], out_r.at[col, rows], local.at[4 + part]).start()

    for i in range(8):
        score(0, i)
    for hp, group in enumerate((early, late)):
        axis_wait(group)
        lax.fori_loop(0, 16, functools.partial(build, hp), 0)
        for i in range(8):
            if hp == 0:
                score(1, i)
            if i > 0:
                attend(hp, i - 1, (i - 1) % 2)
            if hp == 1 and i == 4:
                finish(0)
            soften(hp, i, i % 2)
            if hp == 1 and i == 4:
                send_out(0)
        attend(hp, 7, 1)
    finish(1)
    send_out(1)
    for part in range(2):
        rows = pl.ds(part * 4, 4)
        pltpu.make_async_copy(out_s.at[col, rows], out_r.at[col, rows], local.at[4 + part]).wait()
        whole = remote(out_s.at[pl.ds(0, 15), rows], out_r.at[pl.ds(0, 15), rows], 4 + part, (row, col))
        whole.wait_send()
        whole.wait_recv()

    def place_out(a, b):
        il, group, which, jl = a // 32, lax.rem(a // 8, 4), lax.rem(a // 4, 2), lax.rem(a, 4)
        return b == which * 128 + il * 16 + group * 4 + jl

    back = one_hot((256, 256), place_out)
    blocks = jnp.concatenate([out_r[2 * chip : 2 * chip + 2].reshape(256, 128) for chip in range(8)], axis=1)
    placed = dot(back, blocks).astype(BF16)
    for chip in range(8):
        out_ref[8 * chip : 8 * chip + 8] = placed[:, chip * 128 : chip * 128 + 128].reshape(8, 32, 128)


def body(pair_rep, residue_mask, chain_index, mul_in, mul_gate, mul_out, att_in, att_bias, chain_bias, att_out, trans_up, trans_down):
    vmem = pl.BlockSpec(memory_space=pltpu.VMEM)
    specs = [pl.BlockSpec(memory_space=pl.ANY)] * 12
    specs[8] = pl.BlockSpec(memory_space=pltpu.SMEM)
    sem = pltpu.SemaphoreType
    args = (
        pair_rep, residue_mask.reshape(1, -1), chain_index.reshape(1, -1), mul_in, mul_gate, mul_out, att_in, att_bias.T,
        chain_bias.reshape(1, -1), att_out, trans_up, trans_down,
    )
    return pl.pallas_call(
        kernel,
        out_shape=jax.ShapeDtypeStruct(pair_rep.shape, BF16),
        in_specs=specs,
        out_specs=vmem,
        scratch_shapes=[pltpu.VMEM(a.shape, a.dtype) for n, a in enumerate(args) if n != 8]
        + [
            pltpu.VMEM((2048, 128), F32),
            pltpu.VMEM((4096, 128), F32),
            pltpu.VMEM((128, 2, 16, 128), BF16),
            pltpu.VMEM((128, 2, 16, 128), BF16),
            pltpu.VMEM((512, 512), BF16),
            pltpu.VMEM((512, 512), BF16),
            pltpu.VMEM((2048, 128), F32),
            pltpu.VMEM((128, 16, 128), BF16),
            pltpu.VMEM((128, 16, 128), BF16),
            pltpu.VMEM((16, 4, 32, 128), BF16),
            pltpu.VMEM((8, 512, 128), BF16),
            pltpu.VMEM((4, 512, 128), BF16),
            pltpu.VMEM((4, 4, 4, 2, 8, 128), F32),
            pltpu.VMEM((4, 4, 4, 1, 8, 128), F32),
            pltpu.VMEM((4, 4, 4, 1, 8, 128), F32),
            pltpu.VMEM((4, 4, 4, 2, 8, 128), F32),
            pltpu.VMEM((4, 4, 4, 1, 8, 128), F32),
            pltpu.VMEM((4, 4, 4, 1, 8, 128), F32),
            pltpu.VMEM((4, 256, 512), F32),
            pltpu.VMEM((256, 512), F32),
            pltpu.VMEM((8, 512, 128), BF16),
            pltpu.VMEM((8, 512, 256), BF16),
            pltpu.VMEM((8, 1024, 128), BF16),
            pltpu.VMEM((8, 256, 128), F32),
            pltpu.VMEM((8, 256, 128), F32),
            pltpu.VMEM((2, 8, 512, 512), F32),
            pltpu.VMEM((2, 512, 512), BF16),
            pltpu.VMEM((8, 256, 128), BF16),
            pltpu.VMEM((16, 8, 16, 128), BF16),
            pltpu.VMEM((16, 8, 16, 128), BF16),
            sem.REGULAR((8,)),
            sem.DMA((11,)),
            sem.DMA((8,)),
            sem.DMA((8,)),
            sem.DMA((8,)),
            sem.DMA((6, 2)),
            sem.DMA((6, 2)),
        ],
        compiler_params=pltpu.CompilerParams(collective_id=0, has_side_effects=True, vmem_limit_bytes=56 * 1024 * 1024),
    )(*args)


def solution(mesh):
    in_specs = (P("row", "col", None),) + (P(),) * 11
    return jax.shard_map(body, mesh=mesh, in_specs=in_specs, out_specs=P("row", "col", None), check_vma=False)
```

```python
import functools
import math

import jax
import jax.numpy as jnp
from jax import lax
from jax.experimental import pallas as pl
from jax.experimental.pallas import tpu as pltpu
from jax.sharding import PartitionSpec as P

MESH = pl.DeviceIdType.MESH
F32 = jnp.float32
BF16 = jnp.bfloat16
EPS = 1e-05
LOG2E = math.log2(math.e)
ORDERS = ((0, 1, 2), (1, 2, 0), (2, 0, 1), (1, 2, 0), (0, 1, 2), (2, 0, 1))
WHERE = {(0, 0): (0, 0), (0, 1): (0, 1), (0, 2): (1, 0), (0, 3): (2, 0), (1, 0): (3, 0), (1, 1): (3, 1), (1, 2): (4, 0), (1, 3): (5, 0)}


def norm(values, axis):
    centred = values - jnp.mean(values, axis=axis, keepdims=True)
    variance = jnp.mean(centred * centred, axis=axis, keepdims=True)
    return (centred * lax.rsqrt(variance + EPS)).astype(BF16)


def dot(a, b, ca=1, cb=0):
    return lax.dot_general(a, b, (((ca,), (cb,)), ((), ())), preferred_element_type=F32)


def one_hot(shape, hit):
    rows = lax.broadcasted_iota(jnp.int32, shape, 0)
    cols = lax.broadcasted_iota(jnp.int32, shape, 1)
    return jnp.where(hit(rows, cols), 1.0, 0.0).astype(BF16)


def kernel(
    pair_in, mask_in, chain_in, mul_in_in, mul_gate_in, mul_out_in, att_in_in, att_bias_in, chain_bias_ref,
    att_out_in, up_in, down_in, out_r,
    pair_ref, mask_ref, chain_ref, mul_in_ref, mul_gate_ref, mul_out_ref, att_in_ref, att_bias_ref, att_out_ref, up_ref, down_ref,
    pair_f, lr_f, lr_s, lr_r, at_l, at_r, m_f, m_s, m_r, pair_rows, one_all, normed_all, bias0, bias1, bias2, bias3, bias4, bias5, table, same,
    keys, values, queries, gates, one_mine, score_s, weight_s, gated_s, out_s,
    ready, load, local, send, recv, gather_send, gather_recv,
):
    row, col = lax.axis_index("row"), lax.axis_index("col")
    me = row * 16 + col
    core = lax.rem(col, 2)
    place = (lax.rem(row, 4), col // 8 * 2 + row // 4, lax.rem(col // 2, 4))
    biases = (bias0, bias1, bias2, bias3, bias4, bias5)

    def device_at(c):
        return (lax.rem(c[1], 2) * 4 + c[0], c[1] // 2 * 8 + c[2] * 2 + core)

    def signal_row(sem):
        def one(s, carry):
            pl.semaphore_signal(sem, inc=1, device_id=(lax.rem(row + s, 8), col), device_id_type=MESH)
            return carry
        lax.fori_loop(1, 8, one, 0)

    def signal_col(sem):
        def one(s, carry):
            pl.semaphore_signal(sem, inc=1, device_id=(row, lax.rem(col + s, 16)), device_id_type=MESH)
            return carry
        lax.fori_loop(1, 16, one, 0)

    def remote(src, dst, which, target):
        return pltpu.make_async_remote_copy(src, dst, send.at[which], recv.at[which], device_id=target, device_id_type=MESH)

    loads = [
        pltpu.make_async_copy(src, dst, load.at[n])
        for n, (src, dst) in enumerate((
            (mask_in, mask_ref), (pair_in, pair_ref), (mul_in_in, mul_in_ref), (chain_in, chain_ref),
            (mul_gate_in, mul_gate_ref), (mul_out_in, mul_out_ref), (att_in_in, att_in_ref), (att_bias_in, att_bias_ref),
            (att_out_in, att_out_ref), (up_in, up_ref), (down_in, down_ref),
        ))
    ]
    for one in loads[:3]:
        one.start()
    barrier = pltpu.get_barrier_semaphore()
    signal_row(barrier)
    signal_col(barrier)
    for one in loads[3:]:
        one.start()
    loads[0].wait()

    def send_pair(part):
        rows = pl.ds(2 * part, 2)

        def one(s, carry):
            c = lax.rem(col + s, 16)
            remote(pair_ref.at[pl.ds(4 * c + 2 * part, 2)], pair_rows.at[col, rows], 6 + part, (row, c)).start()
            return carry
        lax.fori_loop(1, 16, one, 0)
        pltpu.make_async_copy(pair_ref.at[pl.ds(4 * col + 2 * part, 2)], pair_rows.at[col, rows], local.at[6 + part]).start()

    mask = mask_ref[...].astype(F32)
    pick_rows = one_hot((512, 128), lambda a, b: a == row * 64 + lax.rem(b, 64))
    row_mask = dot(jnp.broadcast_to(mask, (16, 512)).astype(BF16), pick_rows)
    place_col = lax.broadcasted_iota(jnp.int32, (16, 512), 1) - (col * 32 + 2 * lax.broadcasted_iota(jnp.int32, (16, 512), 0))
    even = jnp.sum(jnp.where(place_col == 0, mask, 0.0), axis=1, keepdims=True)
    odd = jnp.sum(jnp.where(place_col == 1, mask, 0.0), axis=1, keepdims=True)
    lanes16 = lax.broadcasted_iota(jnp.int32, (16, 128), 1)
    pair_mask = jnp.where(lanes16 < 64, even, odd) * row_mask
    loads[1].wait()
    loads[2].wait()
    pair_f[...] = pair_ref[...].astype(F32).reshape(2048, 128)
    mul_in_t = mul_in_ref[...].T
    for step in range(2):
        if step == 1:
            pl.semaphore_wait(barrier, 22)
            for s in range(1, 8):
                pl.semaphore_signal(ready.at[s], inc=1, device_id=(lax.rem(row + s, 8), col), device_id_type=MESH)
            send_pair(0)
        parts = [pair_f[pl.ds(16 * step + u, 64, stride=32), :] for u in range(16)]
        normed = norm(jnp.concatenate(parts, axis=0).T, 0)
        projected = dot(mul_in_t, normed)
        masks = jnp.concatenate([pair_mask[8 * step + v : 8 * step + v + 1] for v in range(8)], axis=1)
        left = masks * jax.nn.sigmoid(projected[128:256]) * projected[:128]
        right = masks * jax.nn.sigmoid(projected[384:]) * projected[256:384]
        for v in range(8):
            lr_f[pl.ds(8 * step + v, 128, stride=32), :] = left[:, v * 128 : v * 128 + 128]
            lr_f[pl.ds(16 + 8 * step + v, 128, stride=32), :] = right[:, v * 128 : v * 128 + 128]
    lr_s[...] = lr_f[...].reshape(128, 2, 16, 128).astype(BF16)

    for one in loads[3:]:
        one.wait()

    def to_row(src, dst, which, s):
        r = lax.rem(row + s, 8)

        def one(n, carry):
            c = lax.rem(col + n, 16)
            remote(src.at[r * 16 + c], dst.at[me], which, (r, c)).start()
            return carry
        lax.fori_loop(1 if s == 0 else 0, 16, one, 0)

    def to_all(src, dst, which):
        for s in range(8):
            if s > 0 and which == 0:
                pl.semaphore_wait(ready.at[8 - s], 1)
            to_row(src, dst, which, s)
        pltpu.make_async_copy(src.at[me], dst.at[me], local.at[which]).start()

    def all_here(src, dst, which):
        pltpu.make_async_copy(src.at[me], dst.at[me], local.at[which]).wait()
        whole = remote(src.at[pl.ds(0, 127)], dst.at[pl.ds(0, 127)], which, (row, col))
        whole.wait_send()
        whole.wait_recv()

    to_all(lr_s, lr_r, 0)

    def place_left(a, b):
        k, il, r, g = b // 128, lax.rem(b // 32, 4), lax.rem(b // 16, 2), lax.rem(b, 16)
        return a == r * 128 + k * 64 + 4 * g + il

    def place_right(a, b):
        k, r, i = b // 128, lax.rem(b // 64, 2), lax.rem(b, 64)
        return a == r * 128 + k * 64 + i

    orders = (one_hot((256, 256), place_left), one_hot((256, 256), place_right))
    head_rows = lax.broadcasted_iota(jnp.int32, (16, 512), 0)
    chains = jnp.where(head_rows == chain_ref[...], 1.0, 0.0).astype(BF16)
    mine = one_hot((256, 512), lambda a, b: b == a // 4 * 8 + core * 4 + lax.rem(a, 4))
    chains_mine = dot(chains, mine, 1, 1).astype(BF16)
    same[...] = dot(chains_mine.T, chains)

    all_here(lr_s, lr_r, 0)

    send_pair(1)
    for side, at in ((0, at_l), (1, at_r)):
        here = [
            jnp.concatenate([lr_r[(2 * rp + o) * 16 : (2 * rp + o + 1) * 16, side].reshape(256, 128) for o in range(2)], axis=1)
            for rp in range(4)
        ]
        turned = dot(jnp.concatenate(here, axis=0), orders[side]).astype(BF16)
        for rp in range(4):
            for k in range(2):
                at[k * 256 : k * 256 + 256, rp * 128 : rp * 128 + 128] = turned[rp * 256 : rp * 256 + 256, k * 128 : k * 128 + 128]
    product = dot(at_l[...], at_r[...], 0, 0)
    for rp in range(4):
        for il in range(4):
            at = rp * 128 + il * 32
            for jt in range(4):
                m_f[pl.ds(rp * 512 + il * 4 + jt, 32, stride=16), :] = product[at : at + 32, jt * 128 : jt * 128 + 128]
    m_s[...] = m_f[...].reshape(128, 16, 128).astype(BF16)
    to_all(m_s, m_r, 2)

    for part in range(2):
        rows = pl.ds(2 * part, 2)
        pltpu.make_async_copy(pair_ref.at[pl.ds(0, 2)], pair_rows.at[0, rows], local.at[6 + part]).wait()
        whole = remote(pair_rows.at[pl.ds(0, 15), rows], pair_rows.at[pl.ds(0, 15), rows], 6 + part, (row, col))
        whole.wait_send()
        whole.wait_recv()

    def pair_block(half):
        blocks = [pair_rows[8 * half : 8 * half + 8, il].reshape(256, 128) for il in range(4)]
        return jnp.concatenate(blocks, axis=0).astype(F32)

    for half in range(2):
        pair_f[half * 1024 : half * 1024 + 1024] = jax.nn.sigmoid(dot(norm(pair_block(half), 1), mul_gate_ref[...]))
    all_here(m_s, m_r, 2)

    early, late = (0, 1, 2), (3, 4, 5)

    def plane_start(which):
        def one(n, carry):
            for o in which:
                a, b, c = ORDERS[o]
                there = list(place)
                there[a] = lax.rem(place[a] + lax.rem(n, 4), 4)
                there[b] = lax.rem(place[b] + n // 4, 4)
                ref = biases[o].at[place[c], place[b], place[a]]
                pltpu.make_async_remote_copy(
                    ref, ref, gather_send.at[o, 0], gather_recv.at[o, 0], device_id=device_at(there), device_id_type=MESH
                ).start()
            return carry
        lax.fori_loop(1, 16, one, 0)

    def plane_wait(which):
        for o in which:
            ref = m_f.at[pl.ds(0, 120 * biases[o].shape[3])]
            whole = pltpu.make_async_remote_copy(
                ref, ref, gather_send.at[o, 0], gather_recv.at[o, 0], device_id=(row, col), device_id_type=MESH
            )
            whole.wait_send()
            whole.wait_recv()

    def axis_start(which):
        for s in (1, 3, 2):
            for o in which:
                c = ORDERS[o][2]
                there = list(place)
                there[c] = lax.rem(place[c] + s, 4)
                ref = biases[o].at[place[c]]
                pltpu.make_async_remote_copy(
                    ref, ref, gather_send.at[o, 1], gather_recv.at[o, 1], device_id=device_at(there), device_id_type=MESH
                ).start()

    def axis_wait(which):
        for o in which:
            ref = biases[o].at[pl.ds(0, 3)]
            whole = pltpu.make_async_remote_copy(
                ref, ref, gather_send.at[o, 1], gather_recv.at[o, 1], device_id=(row, col), device_id_type=MESH
            )
            whole.wait_send()
            whole.wait_recv()

    m_f[...] = m_r[...].astype(F32).reshape(2048, 128)
    bias_in = jnp.concatenate([att_bias_ref[...].astype(F32), jnp.zeros((4, 128), F32)], axis=0).astype(BF16)
    for half in range(2):
        tiles = [m_f[pl.ds(il * 4 + 2 * half + t, 128, stride=16), :] for il in range(4) for t in range(2)]
        update = dot(norm(jnp.concatenate(tiles, axis=1), 0), mul_out_ref[...], 0, 0)
        one = (pair_block(half) + pair_f[half * 1024 : half * 1024 + 1024] * update).astype(BF16)
        normed = norm(one.astype(F32), 1)
        bias = dot(bias_in, normed, 1, 1)
        for il in range(4):
            one_all[core * 4 + il, half * 256 : half * 256 + 256] = one[il * 256 : il * 256 + 256]
            normed_all[il, half * 256 : half * 256 + 256] = normed[il * 256 : il * 256 + 256]
            for t in range(2):
                lanes = slice((il * 2 + t) * 128, (il * 2 + t) * 128 + 128)
                for h in range(4):
                    o, slot = WHERE[h // 2, 2 * half + t]
                    a, b, c = (place[axis] for axis in ORDERS[o])
                    biases[o][c, b, a, slot, h % 2 * 4 + il : h % 2 * 4 + il + 1, :] = bias[h : h + 1, lanes]
        plane_start((0,) if half == 0 else (1, 2))
    plane_start(late)
    sibling = (row, col + 1 - 2 * core)
    swap = remote(one_all.at[pl.ds(core * 4, 4)], one_all.at[pl.ds(core * 4, 4)], 3, sibling)
    swap.start()

    heads = lax.broadcasted_iota(jnp.int32, (256, 128), 1) // 32

    scale = 32 ** (-0.5) * LOG2E

    def project(first, normed):
        four = pl.ds(first, 4)
        kv = dot(normed, att_in_ref[:, 128:384]).astype(BF16)
        keys[four] = kv[:, :128].reshape(4, 512, 128)
        values[four, :, 0:128] = kv[:, 128:].reshape(4, 512, 128)
        values[four, :, 128:256] = jnp.ones((4, 512, 128), BF16)
        picked = []
        for n in range(4):
            both = dot(mine, jnp.concatenate([normed[n * 512 : n * 512 + 512], one_all[first + n]], axis=1))
            picked.append(both[:, :128].astype(BF16))
            one_mine[first + n] = both[:, 128:]
        picked = jnp.concatenate(picked, axis=0)
        query = dot(picked, att_in_ref[:, :128]) * scale
        for n in range(4):
            for h in range(4):
                queries[first + n, h * 256 : h * 256 + 256] = jnp.where(heads == h, query[n * 256 : n * 256 + 256], 0.0).astype(BF16)
        gates[four] = jax.nn.sigmoid(dot(picked, att_in_ref[:, 384:])).reshape(4, 256, 128)

    for o in early:
        plane_wait((o,))
        axis_start((o,))
    project(core * 4, normed_all[...].reshape(2048, 128))
    for o in late:
        plane_wait((o,))
        axis_start((o,))
    swap.wait()
    other = 4 - core * 4
    project(other, norm(one_all[pl.ds(other, 4)].reshape(2048, 128).astype(F32), 1))

    mask_term = 1000000000.0 * (mask - 1.0)
    upper = lax.broadcasted_iota(jnp.int32, (8, 128), 0) < 4

    def build(hp, n, carry):
        x, y = lax.rem(n // 2, 4), lax.rem(n, 2) * 2 + n // 8
        for kt in range(4):
            o, slot = WHERE[hp, kt]
            lanes = pl.ds(kt * 128, 128)
            for zp in range(2):
                tiles = []
                for z in (2 * zp, 2 * zp + 1):
                    at = (x, y, z)
                    a, b, c = (at[axis] for axis in ORDERS[o])
                    tiles.append(biases[o][c, b, a, slot])
                rows = pl.ds(pl.multiple_of(n * 16 + zp * 8, 8), 8)
                together = same[rows, lanes]
                mixed = (
                    jnp.where(upper, tiles[0], pltpu.roll(tiles[1], 4, 0)),
                    jnp.where(upper, pltpu.roll(tiles[0], 4, 0), tiles[1]),
                )
                for h2 in range(2):
                    h = hp * 2 + h2
                    value = mixed[h2] + chain_bias_ref[0, h] * together + mask_term[:, kt * 128 : kt * 128 + 128]
                    table[h, rows, lanes] = value * LOG2E
        return carry


    def score(hp, i):
        score_s[hp, i] = dot(queries[i, hp * 512 : hp * 512 + 512], keys[i], 1, 1)

    def soften(hp, i, slot):
        for n in range(8):
            rows = slice(n * 64, n * 64 + 64)
            scores = score_s[hp, i, rows] + table[2 * hp + n // 4, n % 4 * 64 : n % 4 * 64 + 64]
            weights = jnp.exp2(scores - jnp.max(scores, axis=1, keepdims=True))
            weight_s[slot, rows] = weights.astype(BF16)

    def attend(hp, i, slot):
        weighted = dot(weight_s[slot], values[i])
        weighted = weighted[:, :128] / weighted[:, 128:]
        total = jnp.where(heads == 2 * hp, weighted[:256], jnp.where(heads == 2 * hp + 1, weighted[256:], 0.0))
        gated = (gates[i] * total).astype(BF16)
        gated_s[i] = gated if hp == 0 else jnp.where(heads < 2, gated_s[i], gated)

    def finish(part):
        rows = pl.ds(part * 4, 4)
        two = (one_mine[rows].reshape(1024, 128) + dot(gated_s[rows].reshape(1024, 128), att_out_ref[...])).astype(BF16)
        two_f = two.astype(F32)
        inner = jnp.maximum(dot(norm(two_f, 1), up_ref[...]), 0.0).astype(BF16)
        result = (two_f + dot(inner, down_ref[...])).astype(BF16).reshape(4, 16, 16, 128)
        for n in range(4):
            out_s[:, part * 4 + n] = result[n]

    def send_out(part):
        rows = pl.ds(part * 4, 4)

        def one(s, carry):
            c = lax.rem(col + s, 16)
            remote(out_s.at[c, rows], out_r.at[col, rows], 4 + part, (row, c)).start()
            return carry
        lax.fori_loop(1, 16, one, 0)
        pltpu.make_async_copy(out_s.at[col, rows], out_r.at[col, rows], local.at[4 + part]).start()

    for i in range(8):
        score(0, i)
    for hp, group in enumerate((early, late)):
        axis_wait(group)
        lax.fori_loop(0, 16, functools.partial(build, hp), 0)
        for i in range(8):
            if hp == 0:
                score(1, i)
            if i > 0:
                attend(hp, i - 1, (i - 1) % 2)
            if hp == 1 and i == 4:
                finish(0)
            soften(hp, i, i % 2)
            if hp == 1 and i == 4:
                send_out(0)
        attend(hp, 7, 1)
    finish(1)
    send_out(1)
    for part in range(2):
        rows = pl.ds(part * 4, 4)
        pltpu.make_async_copy(out_s.at[col, rows], out_r.at[col, rows], local.at[4 + part]).wait()
        whole = remote(out_s.at[pl.ds(0, 15), rows], out_r.at[pl.ds(0, 15), rows], 4 + part, (row, col))
        whole.wait_send()
        whole.wait_recv()


def body(pair_rep, residue_mask, chain_index, mul_in, mul_gate, mul_out, att_in, att_bias, chain_bias, att_out, trans_up, trans_down):
    specs = [pl.BlockSpec(memory_space=pl.ANY)] * 12
    specs[8] = pl.BlockSpec(memory_space=pltpu.SMEM)
    sem = pltpu.SemaphoreType
    args = (
        pair_rep, residue_mask.reshape(1, -1), chain_index.reshape(1, -1), mul_in, mul_gate, mul_out, att_in, att_bias.T,
        chain_bias.reshape(1, -1), att_out, trans_up, trans_down,
    )
    parts = pl.pallas_call(
        kernel,
        out_shape=jax.ShapeDtypeStruct((16, 8, 16, 128), BF16),
        in_specs=specs,
        out_specs=pl.BlockSpec(memory_space=pl.ANY),
        scratch_shapes=[pltpu.VMEM(a.shape, a.dtype) for n, a in enumerate(args) if n != 8]
        + [
            pltpu.VMEM((2048, 128), F32),
            pltpu.VMEM((4096, 128), F32),
            pltpu.VMEM((128, 2, 16, 128), BF16),
            pltpu.VMEM((128, 2, 16, 128), BF16),
            pltpu.VMEM((512, 512), BF16),
            pltpu.VMEM((512, 512), BF16),
            pltpu.VMEM((2048, 128), F32),
            pltpu.VMEM((128, 16, 128), BF16),
            pltpu.VMEM((128, 16, 128), BF16),
            pltpu.VMEM((16, 4, 32, 128), BF16),
            pltpu.VMEM((8, 512, 128), BF16),
            pltpu.VMEM((4, 512, 128), BF16),
            pltpu.VMEM((4, 4, 4, 2, 8, 128), F32),
            pltpu.VMEM((4, 4, 4, 1, 8, 128), F32),
            pltpu.VMEM((4, 4, 4, 1, 8, 128), F32),
            pltpu.VMEM((4, 4, 4, 2, 8, 128), F32),
            pltpu.VMEM((4, 4, 4, 1, 8, 128), F32),
            pltpu.VMEM((4, 4, 4, 1, 8, 128), F32),
            pltpu.VMEM((4, 256, 512), F32),
            pltpu.VMEM((256, 512), F32),
            pltpu.VMEM((8, 512, 128), BF16),
            pltpu.VMEM((8, 512, 256), BF16),
            pltpu.VMEM((8, 1024, 128), BF16),
            pltpu.VMEM((8, 256, 128), F32),
            pltpu.VMEM((8, 256, 128), F32),
            pltpu.VMEM((2, 8, 512, 512), F32),
            pltpu.VMEM((2, 512, 512), BF16),
            pltpu.VMEM((8, 256, 128), BF16),
            pltpu.VMEM((16, 8, 16, 128), BF16),
            sem.REGULAR((8,)),
            sem.DMA((11,)),
            sem.DMA((8,)),
            sem.DMA((8,)),
            sem.DMA((8,)),
            sem.DMA((6, 2)),
            sem.DMA((6, 2)),
        ],
        compiler_params=pltpu.CompilerParams(collective_id=0, has_side_effects=True, vmem_limit_bytes=56 * 1024 * 1024),
    )(*args)
    return parts.reshape(8, 2, 8, 4, 4, 128).transpose(0, 2, 3, 1, 4, 5).reshape(pair_rep.shape)


def solution(mesh):
    in_specs = (P("row", "col", None),) + (P(),) * 11
    return jax.shard_map(body, mesh=mesh, in_specs=in_specs, out_specs=P("row", "col", None), check_vma=False)
```

```python
import functools
import math

import jax
import jax.numpy as jnp
from jax import lax
from jax.experimental import pallas as pl
from jax.experimental.pallas import tpu as pltpu
from jax.sharding import PartitionSpec as P

MESH = pl.DeviceIdType.MESH
F32 = jnp.float32
BF16 = jnp.bfloat16
EPS = 1e-05
LOG2E = math.log2(math.e)
ORDERS = ((0, 1, 2), (1, 2, 0), (2, 0, 1), (1, 2, 0), (0, 1, 2), (2, 0, 1))
WHERE = {(0, 0): (0, 0), (0, 1): (0, 1), (0, 2): (1, 0), (0, 3): (2, 0), (1, 0): (3, 0), (1, 1): (3, 1), (1, 2): (4, 0), (1, 3): (5, 0)}


def norm(values, axis):
    centred = values - jnp.mean(values, axis=axis, keepdims=True)
    variance = jnp.mean(centred * centred, axis=axis, keepdims=True)
    return (centred * lax.rsqrt(variance + EPS)).astype(BF16)


def dot(a, b, ca=1, cb=0):
    return lax.dot_general(a, b, (((ca,), (cb,)), ((), ())), preferred_element_type=F32)


def one_hot(shape, hit):
    rows = lax.broadcasted_iota(jnp.int32, shape, 0)
    cols = lax.broadcasted_iota(jnp.int32, shape, 1)
    return jnp.where(hit(rows, cols), 1.0, 0.0).astype(BF16)


def kernel(
    pair_in, mask_in, chain_in, mul_in_in, mul_gate_in, mul_out_in, att_in_in, att_bias_in, chain_bias_ref,
    att_out_in, up_in, down_in, out_r,
    pair_ref, mask_ref, chain_ref, mul_in_ref, mul_gate_ref, mul_out_ref, att_in_ref, att_bias_ref, att_out_ref, up_ref, down_ref,
    pair_f, lr_f, lr_s, lr_r, at_l, at_r, m_f, m_s, m_r, pair_rows, one_all, normed_all, bias0, bias1, bias2, bias3, bias4, bias5, table, same,
    keys, values, queries, gates, one_mine, score_s, weight_s, gated_s, out_s,
    ready, load, local, send, recv, gather_send, gather_recv,
):
    row, col = lax.axis_index("row"), lax.axis_index("col")
    me = row * 16 + col
    core = lax.rem(col, 2)
    place = (lax.rem(row, 4), col // 8 * 2 + row // 4, lax.rem(col // 2, 4))
    biases = (bias0, bias1, bias2, bias3, bias4, bias5)

    def device_at(c):
        return (lax.rem(c[1], 2) * 4 + c[0], c[1] // 2 * 8 + c[2] * 2 + core)

    def signal_row(sem):
        def one(s, carry):
            pl.semaphore_signal(sem, inc=1, device_id=(lax.rem(row + s, 8), col), device_id_type=MESH)
            return carry
        lax.fori_loop(1, 8, one, 0)

    def signal_col(sem):
        def one(s, carry):
            pl.semaphore_signal(sem, inc=1, device_id=(row, lax.rem(col + s, 16)), device_id_type=MESH)
            return carry
        lax.fori_loop(1, 16, one, 0)

    def remote(src, dst, which, target):
        return pltpu.make_async_remote_copy(src, dst, send.at[which], recv.at[which], device_id=target, device_id_type=MESH)

    loads = [
        pltpu.make_async_copy(src, dst, load.at[n])
        for n, (src, dst) in enumerate((
            (mask_in, mask_ref), (pair_in, pair_ref), (mul_in_in, mul_in_ref), (chain_in, chain_ref),
            (mul_gate_in, mul_gate_ref), (mul_out_in, mul_out_ref), (att_in_in, att_in_ref), (att_bias_in, att_bias_ref),
            (att_out_in, att_out_ref), (up_in, up_ref), (down_in, down_ref),
        ))
    ]
    for one in loads[:3]:
        one.start()
    barrier = pltpu.get_barrier_semaphore()
    signal_row(barrier)
    signal_col(barrier)
    for one in loads[3:]:
        one.start()
    loads[0].wait()

    def send_pair(part):
        rows = pl.ds(2 * part, 2)

        def one(s, carry):
            c = lax.rem(col + s, 16)
            remote(pair_ref.at[pl.ds(4 * c + 2 * part, 2)], pair_rows.at[col, rows], 6 + part, (row, c)).start()
            return carry
        lax.fori_loop(1, 16, one, 0)
        pltpu.make_async_copy(pair_ref.at[pl.ds(4 * col + 2 * part, 2)], pair_rows.at[col, rows], local.at[6 + part]).start()

    mask = mask_ref[...].astype(F32)
    pick_rows = one_hot((512, 128), lambda a, b: a == row * 64 + lax.rem(b, 64))
    row_mask = dot(jnp.broadcast_to(mask, (16, 512)).astype(BF16), pick_rows)
    place_col = lax.broadcasted_iota(jnp.int32, (16, 512), 1) - (col * 32 + 2 * lax.broadcasted_iota(jnp.int32, (16, 512), 0))
    even = jnp.sum(jnp.where(place_col == 0, mask, 0.0), axis=1, keepdims=True)
    odd = jnp.sum(jnp.where(place_col == 1, mask, 0.0), axis=1, keepdims=True)
    lanes16 = lax.broadcasted_iota(jnp.int32, (16, 128), 1)
    pair_mask = jnp.where(lanes16 < 64, even, odd) * row_mask
    loads[1].wait()
    loads[2].wait()
    pair_f[...] = pair_ref[...].astype(F32).reshape(2048, 128)
    mul_in_t = mul_in_ref[...].T
    for step in range(2):
        if step == 1:
            pl.semaphore_wait(barrier, 22)
            for s in range(1, 8):
                pl.semaphore_signal(ready.at[s], inc=1, device_id=(lax.rem(row + s, 8), col), device_id_type=MESH)
            send_pair(0)
        parts = [pair_f[pl.ds(16 * step + u, 64, stride=32), :] for u in range(16)]
        normed = norm(jnp.concatenate(parts, axis=0).T, 0)
        projected = dot(mul_in_t, normed)
        masks = jnp.concatenate([pair_mask[8 * step + v : 8 * step + v + 1] for v in range(8)], axis=1)
        left = masks * jax.nn.sigmoid(projected[128:256]) * projected[:128]
        right = masks * jax.nn.sigmoid(projected[384:]) * projected[256:384]
        for v in range(8):
            lr_f[pl.ds(8 * step + v, 128, stride=32), :] = left[:, v * 128 : v * 128 + 128]
            lr_f[pl.ds(16 + 8 * step + v, 128, stride=32), :] = right[:, v * 128 : v * 128 + 128]
    lr_s[...] = lr_f[...].reshape(128, 2, 16, 128).astype(BF16)

    for one in loads[3:]:
        one.wait()

    def to_row(src, dst, which, s):
        r = lax.rem(row + s, 8)

        def one(n, carry):
            c = lax.rem(col + n, 16)
            remote(src.at[r * 16 + c], dst.at[me], which, (r, c)).start()
            return carry
        lax.fori_loop(1 if s == 0 else 0, 16, one, 0)

    def to_all(src, dst, which):
        for s in range(8):
            if s > 0 and which == 0:
                pl.semaphore_wait(ready.at[8 - s], 1)
            to_row(src, dst, which, s)
        pltpu.make_async_copy(src.at[me], dst.at[me], local.at[which]).start()

    def all_here(src, dst, which):
        pltpu.make_async_copy(src.at[me], dst.at[me], local.at[which]).wait()
        whole = remote(src.at[pl.ds(0, 127)], dst.at[pl.ds(0, 127)], which, (row, col))
        whole.wait_send()
        whole.wait_recv()

    to_all(lr_s, lr_r, 0)

    def place_left(a, b):
        k, il, r, g = b // 128, lax.rem(b // 32, 4), lax.rem(b // 16, 2), lax.rem(b, 16)
        return a == r * 128 + k * 64 + 4 * g + il

    def place_right(a, b):
        k, r, i = b // 128, lax.rem(b // 64, 2), lax.rem(b, 64)
        return a == r * 128 + k * 64 + i

    orders = (one_hot((256, 256), place_left), one_hot((256, 256), place_right))
    head_rows = lax.broadcasted_iota(jnp.int32, (16, 512), 0)
    chains = jnp.where(head_rows == chain_ref[...], 1.0, 0.0).astype(BF16)
    mine = one_hot((256, 512), lambda a, b: b == a // 4 * 8 + core * 4 + lax.rem(a, 4))
    chains_mine = dot(chains, mine, 1, 1).astype(BF16)
    same[...] = dot(chains_mine.T, chains)

    all_here(lr_s, lr_r, 0)

    send_pair(1)
    for side, at in ((0, at_l), (1, at_r)):
        here = [
            jnp.concatenate([lr_r[(2 * rp + o) * 16 : (2 * rp + o + 1) * 16, side].reshape(256, 128) for o in range(2)], axis=1)
            for rp in range(4)
        ]
        turned = dot(jnp.concatenate(here, axis=0), orders[side]).astype(BF16)
        for rp in range(4):
            for k in range(2):
                at[k * 256 : k * 256 + 256, rp * 128 : rp * 128 + 128] = turned[rp * 256 : rp * 256 + 256, k * 128 : k * 128 + 128]
    product = dot(at_l[...], at_r[...], 0, 0)
    for rp in range(4):
        for il in range(4):
            at = rp * 128 + il * 32
            for jt in range(4):
                m_f[pl.ds(rp * 512 + il * 4 + jt, 32, stride=16), :] = product[at : at + 32, jt * 128 : jt * 128 + 128]
    m_s[...] = m_f[...].reshape(128, 16, 128).astype(BF16)
    to_all(m_s, m_r, 2)

    for part in range(2):
        rows = pl.ds(2 * part, 2)
        pltpu.make_async_copy(pair_ref.at[pl.ds(0, 2)], pair_rows.at[0, rows], local.at[6 + part]).wait()
        whole = remote(pair_rows.at[pl.ds(0, 15), rows], pair_rows.at[pl.ds(0, 15), rows], 6 + part, (row, col))
        whole.wait_send()
        whole.wait_recv()

    def pair_block(half):
        blocks = [pair_rows[8 * half : 8 * half + 8, il].reshape(256, 128) for il in range(4)]
        return jnp.concatenate(blocks, axis=0).astype(F32)

    for half in range(2):
        pair_f[half * 1024 : half * 1024 + 1024] = jax.nn.sigmoid(dot(norm(pair_block(half), 1), mul_gate_ref[...]))
    all_here(m_s, m_r, 2)

    early, late = (0, 1, 2), (3, 4, 5)

    def plane_start(which):
        def one(n, carry):
            for o in which:
                a, b, c = ORDERS[o]
                there = list(place)
                there[a] = lax.rem(place[a] + lax.rem(n, 4), 4)
                there[b] = lax.rem(place[b] + n // 4, 4)
                ref = biases[o].at[place[c], place[b], place[a]]
                pltpu.make_async_remote_copy(
                    ref, ref, gather_send.at[o, 0], gather_recv.at[o, 0], device_id=device_at(there), device_id_type=MESH
                ).start()
            return carry
        lax.fori_loop(1, 16, one, 0, unroll=True)

    def plane_wait(which):
        for o in which:
            ref = m_f.at[pl.ds(0, 120 * biases[o].shape[3])]
            whole = pltpu.make_async_remote_copy(
                ref, ref, gather_send.at[o, 0], gather_recv.at[o, 0], device_id=(row, col), device_id_type=MESH
            )
            whole.wait_send()
            whole.wait_recv()

    def axis_start(which):
        for s in (1, 3, 2):
            for o in which:
                c = ORDERS[o][2]
                there = list(place)
                there[c] = lax.rem(place[c] + s, 4)
                ref = biases[o].at[place[c]]
                pltpu.make_async_remote_copy(
                    ref, ref, gather_send.at[o, 1], gather_recv.at[o, 1], device_id=device_at(there), device_id_type=MESH
                ).start()

    def axis_wait(which):
        for o in which:
            ref = biases[o].at[pl.ds(0, 3)]
            whole = pltpu.make_async_remote_copy(
                ref, ref, gather_send.at[o, 1], gather_recv.at[o, 1], device_id=(row, col), device_id_type=MESH
            )
            whole.wait_send()
            whole.wait_recv()

    m_f[...] = m_r[...].astype(F32).reshape(2048, 128)
    bias_in = jnp.concatenate([att_bias_ref[...].astype(F32), jnp.zeros((4, 128), F32)], axis=0).astype(BF16)
    for half in range(2):
        tiles = [m_f[pl.ds(il * 4 + 2 * half + t, 128, stride=16), :] for il in range(4) for t in range(2)]
        update = dot(norm(jnp.concatenate(tiles, axis=1), 0), mul_out_ref[...], 0, 0)
        one = (pair_block(half) + pair_f[half * 1024 : half * 1024 + 1024] * update).astype(BF16)
        normed = norm(one.astype(F32), 1)
        bias = dot(bias_in, normed, 1, 1)
        for il in range(4):
            one_all[core * 4 + il, half * 256 : half * 256 + 256] = one[il * 256 : il * 256 + 256]
            normed_all[il, half * 256 : half * 256 + 256] = normed[il * 256 : il * 256 + 256]
            for t in range(2):
                lanes = slice((il * 2 + t) * 128, (il * 2 + t) * 128 + 128)
                for h in range(4):
                    o, slot = WHERE[h // 2, 2 * half + t]
                    a, b, c = (place[axis] for axis in ORDERS[o])
                    biases[o][c, b, a, slot, h % 2 * 4 + il : h % 2 * 4 + il + 1, :] = bias[h : h + 1, lanes]
        plane_start((0,) if half == 0 else (1, 2))
    plane_start(late)
    sibling = (row, col + 1 - 2 * core)
    swap = remote(one_all.at[pl.ds(core * 4, 4)], one_all.at[pl.ds(core * 4, 4)], 3, sibling)
    swap.start()

    heads = lax.broadcasted_iota(jnp.int32, (256, 128), 1) // 32

    scale = 32 ** (-0.5) * LOG2E

    def project(first, normed):
        four = pl.ds(first, 4)
        kv = dot(normed, att_in_ref[:, 128:384]).astype(BF16)
        keys[four] = kv[:, :128].reshape(4, 512, 128)
        values[four, :, 0:128] = kv[:, 128:].reshape(4, 512, 128)
        values[four, :, 128:256] = jnp.ones((4, 512, 128), BF16)
        picked = []
        for n in range(4):
            both = dot(mine, jnp.concatenate([normed[n * 512 : n * 512 + 512], one_all[first + n]], axis=1))
            picked.append(both[:, :128].astype(BF16))
            one_mine[first + n] = both[:, 128:]
        picked = jnp.concatenate(picked, axis=0)
        query = dot(picked, att_in_ref[:, :128]) * scale
        for n in range(4):
            for h in range(4):
                queries[first + n, h * 256 : h * 256 + 256] = jnp.where(heads == h, query[n * 256 : n * 256 + 256], 0.0).astype(BF16)
        gates[four] = jax.nn.sigmoid(dot(picked, att_in_ref[:, 384:])).reshape(4, 256, 128)

    for o in early:
        plane_wait((o,))
        axis_start((o,))
    for o in late:
        plane_wait((o,))
        axis_start((o,))
    project(core * 4, normed_all[...].reshape(2048, 128))
    swap.wait()
    other = 4 - core * 4
    project(other, norm(one_all[pl.ds(other, 4)].reshape(2048, 128).astype(F32), 1))

    mask_term = 1000000000.0 * (mask - 1.0)
    upper = lax.broadcasted_iota(jnp.int32, (8, 128), 0) < 4

    def build(hp, n, carry):
        x, y = lax.rem(n // 2, 4), lax.rem(n, 2) * 2 + n // 8
        for kt in range(4):
            o, slot = WHERE[hp, kt]
            lanes = pl.ds(kt * 128, 128)
            for zp in range(2):
                tiles = []
                for z in (2 * zp, 2 * zp + 1):
                    at = (x, y, z)
                    a, b, c = (at[axis] for axis in ORDERS[o])
                    tiles.append(biases[o][c, b, a, slot])
                rows = pl.ds(pl.multiple_of(n * 16 + zp * 8, 8), 8)
                together = same[rows, lanes]
                mixed = (
                    jnp.where(upper, tiles[0], pltpu.roll(tiles[1], 4, 0)),
                    jnp.where(upper, pltpu.roll(tiles[0], 4, 0), tiles[1]),
                )
                for h2 in range(2):
                    h = hp * 2 + h2
                    value = mixed[h2] + chain_bias_ref[0, h] * together + mask_term[:, kt * 128 : kt * 128 + 128]
                    table[h, rows, lanes] = value * LOG2E
        return carry


    def score(hp, i):
        score_s[hp, i] = dot(queries[i, hp * 512 : hp * 512 + 512], keys[i], 1, 1)

    def soften(hp, i, slot):
        for n in range(8):
            rows = slice(n * 64, n * 64 + 64)
            scores = score_s[hp, i, rows] + table[2 * hp + n // 4, n % 4 * 64 : n % 4 * 64 + 64]
            weights = jnp.exp2(scores - jnp.max(scores, axis=1, keepdims=True))
            weight_s[slot, rows] = weights.astype(BF16)

    def attend(hp, i, slot):
        weighted = dot(weight_s[slot], values[i])
        weighted = weighted[:, :128] / weighted[:, 128:]
        total = jnp.where(heads == 2 * hp, weighted[:256], jnp.where(heads == 2 * hp + 1, weighted[256:], 0.0))
        gated = (gates[i] * total).astype(BF16)
        gated_s[i] = gated if hp == 0 else jnp.where(heads < 2, gated_s[i], gated)

    def finish(part):
        rows = pl.ds(part * 4, 4)
        two = (one_mine[rows].reshape(1024, 128) + dot(gated_s[rows].reshape(1024, 128), att_out_ref[...])).astype(BF16)
        two_f = two.astype(F32)
        inner = jnp.maximum(dot(norm(two_f, 1), up_ref[...]), 0.0).astype(BF16)
        result = (two_f + dot(inner, down_ref[...])).astype(BF16).reshape(4, 16, 16, 128)
        for n in range(4):
            out_s[:, part * 4 + n] = result[n]

    def send_out(part):
        rows = pl.ds(part * 4, 4)

        def one(s, carry):
            c = lax.rem(col + s, 16)
            remote(out_s.at[c, rows], out_r.at[col, rows], 4 + part, (row, c)).start()
            return carry
        lax.fori_loop(1, 16, one, 0, unroll=True)
        pltpu.make_async_copy(out_s.at[col, rows], out_r.at[col, rows], local.at[4 + part]).start()

    for i in range(8):
        score(0, i)
    for hp, group in enumerate((early, late)):
        axis_wait(group)
        lax.fori_loop(0, 16, functools.partial(build, hp), 0, unroll=4)
        for i in range(8):
            if hp == 0:
                score(1, i)
            if i > 0:
                attend(hp, i - 1, (i - 1) % 2)
            if hp == 1 and i == 4:
                finish(0)
            soften(hp, i, i % 2)
            if hp == 1 and i == 4:
                send_out(0)
        attend(hp, 7, 1)
    finish(1)
    send_out(1)
    for part in range(2):
        rows = pl.ds(part * 4, 4)
        pltpu.make_async_copy(out_s.at[col, rows], out_r.at[col, rows], local.at[4 + part]).wait()
        whole = remote(out_s.at[pl.ds(0, 15), rows], out_r.at[pl.ds(0, 15), rows], 4 + part, (row, col))
        whole.wait_send()
        whole.wait_recv()


def body(pair_rep, residue_mask, chain_index, mul_in, mul_gate, mul_out, att_in, att_bias, chain_bias, att_out, trans_up, trans_down):
    specs = [pl.BlockSpec(memory_space=pl.ANY)] * 12
    specs[8] = pl.BlockSpec(memory_space=pltpu.SMEM)
    sem = pltpu.SemaphoreType
    args = (
        pair_rep, residue_mask.reshape(1, -1), chain_index.reshape(1, -1), mul_in, mul_gate, mul_out, att_in, att_bias.T,
        chain_bias.reshape(1, -1), att_out, trans_up, trans_down,
    )
    parts = pl.pallas_call(
        kernel,
        out_shape=jax.ShapeDtypeStruct((16, 8, 16, 128), BF16),
        in_specs=specs,
        out_specs=pl.BlockSpec(memory_space=pl.ANY),
        scratch_shapes=[pltpu.VMEM(a.shape, a.dtype) for n, a in enumerate(args) if n != 8]
        + [
            pltpu.VMEM((2048, 128), F32),
            pltpu.VMEM((4096, 128), F32),
            pltpu.VMEM((128, 2, 16, 128), BF16),
            pltpu.VMEM((128, 2, 16, 128), BF16),
            pltpu.VMEM((512, 512), BF16),
            pltpu.VMEM((512, 512), BF16),
            pltpu.VMEM((2048, 128), F32),
            pltpu.VMEM((128, 16, 128), BF16),
            pltpu.VMEM((128, 16, 128), BF16),
            pltpu.VMEM((16, 4, 32, 128), BF16),
            pltpu.VMEM((8, 512, 128), BF16),
            pltpu.VMEM((4, 512, 128), BF16),
            pltpu.VMEM((4, 4, 4, 2, 8, 128), F32),
            pltpu.VMEM((4, 4, 4, 1, 8, 128), F32),
            pltpu.VMEM((4, 4, 4, 1, 8, 128), F32),
            pltpu.VMEM((4, 4, 4, 2, 8, 128), F32),
            pltpu.VMEM((4, 4, 4, 1, 8, 128), F32),
            pltpu.VMEM((4, 4, 4, 1, 8, 128), F32),
            pltpu.VMEM((4, 256, 512), F32),
            pltpu.VMEM((256, 512), F32),
            pltpu.VMEM((8, 512, 128), BF16),
            pltpu.VMEM((8, 512, 256), BF16),
            pltpu.VMEM((8, 1024, 128), BF16),
            pltpu.VMEM((8, 256, 128), F32),
            pltpu.VMEM((8, 256, 128), F32),
            pltpu.VMEM((2, 8, 512, 512), F32),
            pltpu.VMEM((2, 512, 512), BF16),
            pltpu.VMEM((8, 256, 128), BF16),
            pltpu.VMEM((16, 8, 16, 128), BF16),
            sem.REGULAR((8,)),
            sem.DMA((11,)),
            sem.DMA((8,)),
            sem.DMA((8,)),
            sem.DMA((8,)),
            sem.DMA((6, 2)),
            sem.DMA((6, 2)),
        ],
        compiler_params=pltpu.CompilerParams(collective_id=0, has_side_effects=True, vmem_limit_bytes=56 * 1024 * 1024),
    )(*args)
    return parts.reshape(8, 2, 8, 4, 4, 128).transpose(0, 2, 3, 1, 4, 5).reshape(pair_rep.shape)


def solution(mesh):
    in_specs = (P("row", "col", None),) + (P(),) * 11
    return jax.shard_map(body, mesh=mesh, in_specs=in_specs, out_specs=P("row", "col", None), check_vma=False)
```

```python
import functools
import math

import jax
import jax.numpy as jnp
from jax import lax
from jax.experimental import pallas as pl
from jax.experimental.pallas import tpu as pltpu
from jax.sharding import PartitionSpec as P

MESH = pl.DeviceIdType.MESH
F32 = jnp.float32
BF16 = jnp.bfloat16
EPS = 1e-05
LOG2E = math.log2(math.e)
ORDERS = ((0, 1, 2), (1, 2, 0), (2, 0, 1), (1, 2, 0), (0, 1, 2), (2, 0, 1))
WHERE = {(0, 0): (0, 0), (0, 1): (0, 1), (0, 2): (1, 0), (0, 3): (2, 0), (1, 0): (3, 0), (1, 1): (3, 1), (1, 2): (4, 0), (1, 3): (5, 0)}


def norm(values, axis):
    centred = values - jnp.mean(values, axis=axis, keepdims=True)
    variance = jnp.mean(centred * centred, axis=axis, keepdims=True)
    return (centred * lax.rsqrt(variance + EPS)).astype(BF16)


def dot(a, b, ca=1, cb=0):
    return lax.dot_general(a, b, (((ca,), (cb,)), ((), ())), preferred_element_type=F32)


def one_hot(shape, hit):
    rows = lax.broadcasted_iota(jnp.int32, shape, 0)
    cols = lax.broadcasted_iota(jnp.int32, shape, 1)
    return jnp.where(hit(rows, cols), 1.0, 0.0).astype(BF16)


def kernel(
    pair_in, mask_in, chain_in, mul_in_in, mul_gate_in, mul_out_in, att_in_in, att_bias_in, chain_bias_ref,
    att_out_in, up_in, down_in, out_r,
    pair_ref, mask_ref, chain_ref, mul_in_ref, mul_gate_ref, mul_out_ref, att_in_ref, att_bias_ref, att_out_ref, up_ref, down_ref,
    pair_f, lr_f, lr_s, lr_r, at_l, at_r, m_f, m_s, m_r, pair_rows, one_all, normed_all, bias0, bias1, bias2, bias3, bias4, bias5, table, same,
    keys, values, queries, gates, one_mine, score_s, weight_s, gated_s, out_s,
    ready, load, local, send, recv, gather_send, gather_recv,
):
    row, col = lax.axis_index("row"), lax.axis_index("col")
    me = row * 16 + col
    core = lax.rem(col, 2)
    place = (lax.rem(row, 4), col // 8 * 2 + row // 4, lax.rem(col // 2, 4))
    biases = (bias0, bias1, bias2, bias3, bias4, bias5)

    def device_at(c):
        return (lax.rem(c[1], 2) * 4 + c[0], c[1] // 2 * 8 + c[2] * 2 + core)

    def signal_row(sem):
        def one(s, carry):
            pl.semaphore_signal(sem, inc=1, device_id=(lax.rem(row + s, 8), col), device_id_type=MESH)
            return carry
        lax.fori_loop(1, 8, one, 0)

    def signal_col(sem):
        def one(s, carry):
            pl.semaphore_signal(sem, inc=1, device_id=(row, lax.rem(col + s, 16)), device_id_type=MESH)
            return carry
        lax.fori_loop(1, 16, one, 0)

    def remote(src, dst, which, target):
        return pltpu.make_async_remote_copy(src, dst, send.at[which], recv.at[which], device_id=target, device_id_type=MESH)

    loads = [
        pltpu.make_async_copy(src, dst, load.at[n])
        for n, (src, dst) in enumerate((
            (mask_in, mask_ref), (pair_in, pair_ref), (mul_in_in, mul_in_ref), (chain_in, chain_ref),
            (mul_gate_in, mul_gate_ref), (mul_out_in, mul_out_ref), (att_in_in, att_in_ref), (att_bias_in, att_bias_ref),
            (att_out_in, att_out_ref), (up_in, up_ref), (down_in, down_ref),
        ))
    ]
    for one in loads[:3]:
        one.start()
    barrier = pltpu.get_barrier_semaphore()
    signal_row(barrier)
    signal_col(barrier)
    for one in loads[3:]:
        one.start()
    loads[0].wait()

    def send_pair(part):
        rows = pl.ds(2 * part, 2)

        def one(s, carry):
            c = lax.rem(col + s, 16)
            remote(pair_ref.at[pl.ds(4 * c + 2 * part, 2)], pair_rows.at[col, rows], 6 + part, (row, c)).start()
            return carry
        lax.fori_loop(1, 16, one, 0)
        pltpu.make_async_copy(pair_ref.at[pl.ds(4 * col + 2 * part, 2)], pair_rows.at[col, rows], local.at[6 + part]).start()

    mask = mask_ref[...].astype(F32)
    pick_rows = one_hot((512, 128), lambda a, b: a == row * 64 + lax.rem(b, 64))
    row_mask = dot(jnp.broadcast_to(mask, (16, 512)).astype(BF16), pick_rows)
    place_col = lax.broadcasted_iota(jnp.int32, (16, 512), 1) - (col * 32 + 2 * lax.broadcasted_iota(jnp.int32, (16, 512), 0))
    even = jnp.sum(jnp.where(place_col == 0, mask, 0.0), axis=1, keepdims=True)
    odd = jnp.sum(jnp.where(place_col == 1, mask, 0.0), axis=1, keepdims=True)
    lanes16 = lax.broadcasted_iota(jnp.int32, (16, 128), 1)
    pair_mask = jnp.where(lanes16 < 64, even, odd) * row_mask
    loads[1].wait()
    loads[2].wait()
    pair_f[0:2048] = pair_ref[...].astype(F32).reshape(2048, 128)
    mul_in_t = mul_in_ref[...].T
    for step in range(2):
        if step == 1:
            pl.semaphore_wait(barrier, 22)
            for s in range(1, 8):
                pl.semaphore_signal(ready.at[s], inc=1, device_id=(lax.rem(row + s, 8), col), device_id_type=MESH)
            send_pair(0)
        parts = [pair_f[pl.ds(16 * step + u, 64, stride=32), :] for u in range(16)]
        normed = norm(jnp.concatenate(parts, axis=0).T, 0)
        projected = dot(mul_in_t, normed)
        masks = jnp.concatenate([pair_mask[8 * step + v : 8 * step + v + 1] for v in range(8)], axis=1)
        left = masks * jax.nn.sigmoid(projected[128:256]) * projected[:128]
        right = masks * jax.nn.sigmoid(projected[384:]) * projected[256:384]
        for v in range(8):
            lr_f[pl.ds(8 * step + v, 128, stride=32), :] = left[:, v * 128 : v * 128 + 128]
            lr_f[pl.ds(16 + 8 * step + v, 128, stride=32), :] = right[:, v * 128 : v * 128 + 128]
    lr_s[...] = lr_f[0:4096].reshape(128, 2, 16, 128).astype(BF16)

    for one in loads[3:]:
        one.wait()

    def to_row(src, dst, which, s):
        r = lax.rem(row + s, 8)

        def one(n, carry):
            c = lax.rem(col + n, 16)
            remote(src.at[r * 16 + c], dst.at[me], which, (r, c)).start()
            return carry
        lax.fori_loop(1 if s == 0 else 0, 16, one, 0)

    def to_all(src, dst, which):
        for s in range(8):
            if s > 0 and which == 0:
                pl.semaphore_wait(ready.at[8 - s], 1)
            to_row(src, dst, which, s)
        pltpu.make_async_copy(src.at[me], dst.at[me], local.at[which]).start()

    def all_here(src, dst, which):
        pltpu.make_async_copy(src.at[me], dst.at[me], local.at[which]).wait()
        whole = remote(src.at[pl.ds(0, 127)], dst.at[pl.ds(0, 127)], which, (row, col))
        whole.wait_send()
        whole.wait_recv()

    to_all(lr_s, lr_r, 0)

    def place_left(a, b):
        k, il, r, g = b // 128, lax.rem(b // 32, 4), lax.rem(b // 16, 2), lax.rem(b, 16)
        return a == r * 128 + k * 64 + 4 * g + il

    def place_right(a, b):
        k, r, i = b // 128, lax.rem(b // 64, 2), lax.rem(b, 64)
        return a == r * 128 + k * 64 + i

    orders = (one_hot((256, 256), place_left), one_hot((256, 256), place_right))
    head_rows = lax.broadcasted_iota(jnp.int32, (16, 512), 0)
    chains = jnp.where(head_rows == chain_ref[...], 1.0, 0.0).astype(BF16)
    mine = one_hot((256, 512), lambda a, b: b == a // 4 * 8 + core * 4 + lax.rem(a, 4))
    chains_mine = dot(chains, mine, 1, 1).astype(BF16)
    same[...] = dot(chains_mine.T, chains)

    all_here(lr_s, lr_r, 0)

    send_pair(1)
    for side, at in ((0, at_l), (1, at_r)):
        here = [
            jnp.concatenate([lr_r[(2 * rp + o) * 16 : (2 * rp + o + 1) * 16, side].reshape(256, 128) for o in range(2)], axis=1)
            for rp in range(4)
        ]
        turned = dot(jnp.concatenate(here, axis=0), orders[side]).astype(BF16)
        for rp in range(4):
            for k in range(2):
                at[k * 256 : k * 256 + 256, rp * 128 : rp * 128 + 128] = turned[rp * 256 : rp * 256 + 256, k * 128 : k * 128 + 128]
    product = dot(at_l[...], at_r[...], 0, 0)
    for rp in range(4):
        for il in range(4):
            at = rp * 128 + il * 32
            for jt in range(4):
                m_f[pl.ds(rp * 512 + il * 4 + jt, 32, stride=16), :] = product[at : at + 32, jt * 128 : jt * 128 + 128]
    m_s[...] = m_f[0:2048].reshape(128, 16, 128).astype(BF16)
    to_all(m_s, m_r, 2)

    for part in range(2):
        rows = pl.ds(2 * part, 2)
        pltpu.make_async_copy(pair_ref.at[pl.ds(0, 2)], pair_rows.at[0, rows], local.at[6 + part]).wait()
        whole = remote(pair_rows.at[pl.ds(0, 15), rows], pair_rows.at[pl.ds(0, 15), rows], 6 + part, (row, col))
        whole.wait_send()
        whole.wait_recv()

    def pair_block(half):
        blocks = [pair_rows[8 * half : 8 * half + 8, il].reshape(256, 128) for il in range(4)]
        return jnp.concatenate(blocks, axis=0).astype(F32)

    for half in range(2):
        pair_f[half * 1024 : half * 1024 + 1024] = jax.nn.sigmoid(dot(norm(pair_block(half), 1), mul_gate_ref[...]))
    all_here(m_s, m_r, 2)

    early, late = (0, 1, 2), (3, 4, 5)

    def plane_start(which):
        def one(n, carry):
            for o in which:
                a, b, c = ORDERS[o]
                there = list(place)
                there[a] = lax.rem(place[a] + lax.rem(n, 4), 4)
                there[b] = lax.rem(place[b] + n // 4, 4)
                ref = biases[o].at[place[c], place[b], place[a]]
                pltpu.make_async_remote_copy(
                    ref, ref, gather_send.at[o, 0], gather_recv.at[o, 0], device_id=device_at(there), device_id_type=MESH
                ).start()
            return carry
        lax.fori_loop(1, 16, one, 0, unroll=True)

    def plane_wait(which):
        for o in which:
            ref = m_f.at[pl.ds(0, 120 * biases[o].shape[3])]
            whole = pltpu.make_async_remote_copy(
                ref, ref, gather_send.at[o, 0], gather_recv.at[o, 0], device_id=(row, col), device_id_type=MESH
            )
            whole.wait_send()
            whole.wait_recv()

    def axis_start(which):
        for s in (1, 3, 2):
            for o in which:
                c = ORDERS[o][2]
                there = list(place)
                there[c] = lax.rem(place[c] + s, 4)
                ref = biases[o].at[place[c]]
                pltpu.make_async_remote_copy(
                    ref, ref, gather_send.at[o, 1], gather_recv.at[o, 1], device_id=device_at(there), device_id_type=MESH
                ).start()

    def axis_wait(which):
        for o in which:
            ref = biases[o].at[pl.ds(0, 3)]
            whole = pltpu.make_async_remote_copy(
                ref, ref, gather_send.at[o, 1], gather_recv.at[o, 1], device_id=(row, col), device_id_type=MESH
            )
            whole.wait_send()
            whole.wait_recv()

    m_f[0:2048] = m_r[...].astype(F32).reshape(2048, 128)
    bias_in = jnp.concatenate([att_bias_ref[...].astype(F32), jnp.zeros((4, 128), F32)], axis=0).astype(BF16)
    for half in range(2):
        tiles = [m_f[pl.ds(il * 4 + 2 * half + t, 128, stride=16), :] for il in range(4) for t in range(2)]
        update = dot(norm(jnp.concatenate(tiles, axis=1), 0), mul_out_ref[...], 0, 0)
        one = (pair_block(half) + pair_f[half * 1024 : half * 1024 + 1024] * update).astype(BF16)
        normed = norm(one.astype(F32), 1)
        bias = dot(bias_in, normed, 1, 1)
        for il in range(4):
            one_all[core * 4 + il, half * 256 : half * 256 + 256] = one[il * 256 : il * 256 + 256]
            normed_all[il, half * 256 : half * 256 + 256] = normed[il * 256 : il * 256 + 256]
            for t in range(2):
                lanes = slice((il * 2 + t) * 128, (il * 2 + t) * 128 + 128)
                for h in range(4):
                    o, slot = WHERE[h // 2, 2 * half + t]
                    a, b, c = (place[axis] for axis in ORDERS[o])
                    biases[o][c, b, a, slot, h % 2 * 4 + il : h % 2 * 4 + il + 1, :] = bias[h : h + 1, lanes]
        plane_start((0,) if half == 0 else (1, 2))
    plane_start(late)
    sibling = (row, col + 1 - 2 * core)
    swap = remote(one_all.at[pl.ds(core * 4, 4)], one_all.at[pl.ds(core * 4, 4)], 3, sibling)
    swap.start()

    heads = lax.broadcasted_iota(jnp.int32, (256, 128), 1) // 32

    scale = 32 ** (-0.5) * LOG2E

    def project(first, normed):
        four = pl.ds(first, 4)
        kv = dot(normed, att_in_ref[:, 128:384]).astype(BF16)
        keys[four] = kv[:, :128].reshape(4, 512, 128)
        values[four, :, 0:128] = kv[:, 128:].reshape(4, 512, 128)
        values[four, :, 128:256] = jnp.ones((4, 512, 128), BF16)
        picked = []
        for n in range(4):
            both = dot(mine, jnp.concatenate([normed[n * 512 : n * 512 + 512], one_all[first + n]], axis=1))
            picked.append(both[:, :128].astype(BF16))
            one_mine[first + n] = both[:, 128:]
        picked = jnp.concatenate(picked, axis=0)
        query = dot(picked, att_in_ref[:, :128]) * scale
        for n in range(4):
            for h in range(4):
                queries[first + n, h * 256 : h * 256 + 256] = jnp.where(heads == h, query[n * 256 : n * 256 + 256], 0.0).astype(BF16)
        gates[four] = jax.nn.sigmoid(dot(picked, att_in_ref[:, 384:])).reshape(4, 256, 128)

    for o in early:
        plane_wait((o,))
        axis_start((o,))
    for o in late:
        plane_wait((o,))
        axis_start((o,))
    project(core * 4, normed_all[...].reshape(2048, 128))
    swap.wait()
    other = 4 - core * 4
    project(other, norm(one_all[pl.ds(other, 4)].reshape(2048, 128).astype(F32), 1))

    mask_term = 1000000000.0 * (mask - 1.0)
    upper = lax.broadcasted_iota(jnp.int32, (8, 128), 0) < 4

    def build(hp, n, carry):
        x, y = lax.rem(n // 2, 4), lax.rem(n, 2) * 2 + n // 8
        for kt in range(4):
            o, slot = WHERE[hp, kt]
            lanes = pl.ds(kt * 128, 128)
            for zp in range(2):
                tiles = []
                for z in (2 * zp, 2 * zp + 1):
                    at = (x, y, z)
                    a, b, c = (at[axis] for axis in ORDERS[o])
                    tiles.append(biases[o][c, b, a, slot])
                rows = pl.ds(pl.multiple_of(n * 16 + zp * 8, 8), 8)
                together = same[rows, lanes]
                mixed = (
                    jnp.where(upper, tiles[0], pltpu.roll(tiles[1], 4, 0)),
                    jnp.where(upper, pltpu.roll(tiles[0], 4, 0), tiles[1]),
                )
                for h2 in range(2):
                    h = hp * 2 + h2
                    value = mixed[h2] + chain_bias_ref[0, h] * together + mask_term[:, kt * 128 : kt * 128 + 128]
                    table[h, rows, lanes] = value * LOG2E
        return carry


    def score(hp, i):
        score_s[hp, i] = dot(queries[i, hp * 512 : hp * 512 + 512], keys[i], 1, 1)

    def soften(hp, i, slot):
        for n in range(8):
            rows = slice(n * 64, n * 64 + 64)
            scores = score_s[hp, i, rows] + table[2 * hp + n // 4, n % 4 * 64 : n % 4 * 64 + 64]
            weights = jnp.exp2(scores - jnp.max(scores, axis=1, keepdims=True))
            weight_s[slot, rows] = weights.astype(BF16)

    def attend(hp, i, slot):
        weighted = dot(weight_s[slot], values[i])
        weighted = weighted[:, :128] / weighted[:, 128:]
        total = jnp.where(heads == 2 * hp, weighted[:256], jnp.where(heads == 2 * hp + 1, weighted[256:], 0.0))
        gated = (gates[i] * total).astype(BF16)
        gated_s[i] = gated if hp == 0 else jnp.where(heads < 2, gated_s[i], gated)

    def finish(part):
        rows = pl.ds(part * 4, 4)
        two = (one_mine[rows].reshape(1024, 128) + dot(gated_s[rows].reshape(1024, 128), att_out_ref[...])).astype(BF16)
        two_f = two.astype(F32)
        inner = jnp.maximum(dot(norm(two_f, 1), up_ref[...]), 0.0).astype(BF16)
        result = (two_f + dot(inner, down_ref[...])).astype(BF16).reshape(4, 16, 16, 128)
        for n in range(4):
            out_s[:, part * 4 + n] = result[n]

    def send_out(part):
        rows = pl.ds(part * 4, 4)

        def one(s, carry):
            c = lax.rem(col + s, 16)
            remote(out_s.at[c, rows], out_r.at[col, rows], 4 + part, (row, c)).start()
            return carry
        lax.fori_loop(1, 16, one, 0, unroll=True)
        pltpu.make_async_copy(out_s.at[col, rows], out_r.at[col, rows], local.at[4 + part]).start()

    for i in range(8):
        score(0, i)
    for hp, group in enumerate((early, late)):
        axis_wait(group)
        lax.fori_loop(0, 16, functools.partial(build, hp), 0, unroll=4)
        for i in range(8):
            if hp == 0:
                score(1, i)
            if i > 0:
                attend(hp, i - 1, (i - 1) % 2)
            if hp == 1 and i == 4:
                finish(0)
            soften(hp, i, i % 2)
            if hp == 1 and i == 4:
                send_out(0)
        attend(hp, 7, 1)
    finish(1)
    send_out(1)
    for part in range(2):
        rows = pl.ds(part * 4, 4)
        pltpu.make_async_copy(out_s.at[col, rows], out_r.at[col, rows], local.at[4 + part]).wait()
        whole = remote(out_s.at[pl.ds(0, 15), rows], out_r.at[pl.ds(0, 15), rows], 4 + part, (row, col))
        whole.wait_send()
        whole.wait_recv()


def body(pair_rep, residue_mask, chain_index, mul_in, mul_gate, mul_out, att_in, att_bias, chain_bias, att_out, trans_up, trans_down):
    specs = [pl.BlockSpec(memory_space=pl.ANY)] * 12
    specs[8] = pl.BlockSpec(memory_space=pltpu.SMEM)
    sem = pltpu.SemaphoreType
    args = (
        pair_rep, residue_mask.reshape(1, -1), chain_index.reshape(1, -1), mul_in, mul_gate, mul_out, att_in, att_bias.T,
        chain_bias.reshape(1, -1), att_out, trans_up, trans_down,
    )
    parts = pl.pallas_call(
        kernel,
        out_shape=jax.ShapeDtypeStruct((16, 8, 16, 128), BF16),
        in_specs=specs,
        out_specs=pl.BlockSpec(memory_space=pl.ANY),
        scratch_shapes=[pltpu.VMEM(a.shape, a.dtype) for n, a in enumerate(args) if n != 8]
        + [
            pltpu.VMEM((2080, 128), F32),
            pltpu.VMEM((4128, 128), F32),
            pltpu.VMEM((128, 2, 16, 128), BF16),
            pltpu.VMEM((128, 2, 16, 128), BF16),
            pltpu.VMEM((512, 512), BF16),
            pltpu.VMEM((512, 512), BF16),
            pltpu.VMEM((2080, 128), F32),
            pltpu.VMEM((128, 16, 128), BF16),
            pltpu.VMEM((128, 16, 128), BF16),
            pltpu.VMEM((16, 4, 32, 128), BF16),
            pltpu.VMEM((8, 512, 128), BF16),
            pltpu.VMEM((4, 512, 128), BF16),
            pltpu.VMEM((4, 4, 4, 2, 8, 128), F32),
            pltpu.VMEM((4, 4, 4, 1, 8, 128), F32),
            pltpu.VMEM((4, 4, 4, 1, 8, 128), F32),
            pltpu.VMEM((4, 4, 4, 2, 8, 128), F32),
            pltpu.VMEM((4, 4, 4, 1, 8, 128), F32),
            pltpu.VMEM((4, 4, 4, 1, 8, 128), F32),
            pltpu.VMEM((4, 256, 512), F32),
            pltpu.VMEM((256, 512), F32),
            pltpu.VMEM((8, 512, 128), BF16),
            pltpu.VMEM((8, 512, 256), BF16),
            pltpu.VMEM((8, 1024, 128), BF16),
            pltpu.VMEM((8, 256, 128), F32),
            pltpu.VMEM((8, 256, 128), F32),
            pltpu.VMEM((2, 8, 512, 512), F32),
            pltpu.VMEM((2, 512, 512), BF16),
            pltpu.VMEM((8, 256, 128), BF16),
            pltpu.VMEM((16, 8, 16, 128), BF16),
            sem.REGULAR((8,)),
            sem.DMA((11,)),
            sem.DMA((8,)),
            sem.DMA((8,)),
            sem.DMA((8,)),
            sem.DMA((6, 2)),
            sem.DMA((6, 2)),
        ],
        compiler_params=pltpu.CompilerParams(collective_id=0, has_side_effects=True, vmem_limit_bytes=56 * 1024 * 1024),
    )(*args)
    return parts.reshape(8, 2, 8, 4, 4, 128).transpose(0, 2, 3, 1, 4, 5).reshape(pair_rep.shape)


def solution(mesh):
    in_specs = (P("row", "col", None),) + (P(),) * 11
    return jax.shard_map(body, mesh=mesh, in_specs=in_specs, out_specs=P("row", "col", None), check_vma=False)
```
